256 devices in a mesh: dp: 4 (over x), mp: 64 (over y, z, core).
Axes of the slice: x: 4, y: 4, z: 8, core: 2. Of those that a mesh axis runs over, the one named last changes fastest.
Arguments:
- tokens: bfloat16 [1024, 8192], P('dp', 'mp'), may hold values from -6 to 6
- cotangent: bfloat16 [1024, 8192], P('dp', 'mp'), may hold values from -6 to 6
- weight_codes: int32 [192, 48, 128, 128], P('mp'), may hold values from 0 to 4095
- block_scales: float32 [3, 192, 48, 128], P(None, 'mp'), may hold values from 0.0011 to 0.01
- block_index: int32 [192, 48], P('mp'), may hold values from 0 to 63, as said below
- block_count: int32 [192], P('mp'), may hold values from 16 to 48, as said below
- ia3_scale: float32 [24576], P('mp'), may hold values from 0.1 to 1.9
Outputs:
- input_grad: bfloat16 [1024, 8192], P('dp', 'mp')
- ia3_grad: float32 [24576], P('mp')
The draws below stay inside these ranges and needn't reach their ends.
Inputs may be any that keep to these rules, and one draw needn't show every extreme that they name: `block_index`: each row holds 48 different block numbers; only its first block_count entries are live. `block_count`: some hidden block has exactly 48 live slots and another exactly 16.
All inputs are finite; a program needn't handle non-finite values.
Results may differ from the reference program's by a relative error of at most 0.0072.
Values may be sent and summed in bfloat16 or wider, within the bound.
No kernel may reach another device: no remote copies, remote signals or barrier semaphores. Data moves between devices by JAX's collectives and lax.ppermute only.
A program may use at most 128 MiB of HBM per device.

```python
import math
import jax
import jax.numpy as jnp
from jax import lax

D = 8192
BLK = 128
KMAX = 48
KMIN = 16
HID_BLOCKS = 192
FF = 24576
TOKENS = 1024


def pattern_parts(key):
    blocks = D // BLK
    row_keys = jax.random.split(jax.random.fold_in(key, 11), HID_BLOCKS)
    orders = jax.vmap(lambda row_key: jax.random.permutation(row_key, blocks))(row_keys)
    index_table = orders[:, :KMAX].astype(jnp.int32)
    counts = jax.random.randint(jax.random.fold_in(key, 12), (HID_BLOCKS,), KMIN, KMAX + 1).astype(jnp.int32)
    fullest = jax.random.randint(jax.random.fold_in(key, 13), (), 0, HID_BLOCKS)
    offset = jax.random.randint(jax.random.fold_in(key, 14), (), 0, HID_BLOCKS - 1)
    emptiest = (fullest + 1 + offset) % HID_BLOCKS
    counts = counts.at[fullest].set(KMAX).at[emptiest].set(KMIN)
    return (index_table, counts)


def draw_block_index(key, part):
    return pattern_parts(key)[0]


def draw_block_count(key, part):
    return pattern_parts(key)[1]


def plant(array, stream_key, low, high):
    dims = array.shape
    index_at = [jax.random.randint(jax.random.fold_in(stream_key, axis), (), 0, dims[axis]) for axis in range(len(dims))]
    array = array.at[tuple(index_at)].set(low)
    longest = dims.index(max(dims))
    index_at[longest] = (index_at[longest] + 1) % dims[longest]
    return array.at[tuple(index_at)].set(high)


def shard_levels(own_key, extent, pieces, smallest, high):
    def one(dim, parts):
        draws = jax.random.uniform(jax.random.fold_in(jax.random.fold_in(own_key, 6), dim), (parts,), jnp.float32, smallest / len(pieces), high / len(pieces))
        return jnp.repeat(jnp.exp(draws), extent[dim] // parts).reshape((-1,) + (1,) * (len(extent) - dim - 1))

    factor_of = one(*pieces[0])
    for cut in pieces[1:]:
        factor_of = factor_of * one(*cut)
    return factor_of


def gaussian(rng, dims, deviation, limit, cuts=(), held_as=jnp.bfloat16):
    factor_of = shard_levels(rng, dims, cuts, -0.22, 0.18) if cuts else 1.0
    values = jax.random.normal(rng, dims, jnp.float32) * deviation * factor_of
    return jnp.minimum(jnp.maximum(values, -limit), limit).astype(held_as)


def setup_inputs(seed: int = 0) -> dict:
    keys = jax.random.split(jax.random.key(seed), 8)
    tokens = gaussian(keys[0], (TOKENS, D), 1.0, 6.0, ((0, 4), (1, 64)))
    cotangent = gaussian(keys[1], (TOKENS, D), 1.0, 6.0, ((0, 4), (1, 64)))
    weight_codes = plant(jax.random.randint(keys[2], (HID_BLOCKS, KMAX, BLK, BLK), 0, 4096), jax.random.fold_in(keys[2], 1), 0, 4095).astype(jnp.int32)
    block_scales = jnp.clip(jnp.exp(math.log(0.01) - 2.207275 * jax.random.uniform(keys[3], (3, HID_BLOCKS, KMAX, BLK), jnp.float32) ** shard_levels(keys[3], (3, HID_BLOCKS, KMAX, BLK), ((1, 64),), -0.2, 0.2)), 0.0011, 0.01)
    block_index = draw_block_index(jax.random.fold_in(keys[7], 71), 0)
    block_count = draw_block_count(jax.random.fold_in(keys[7], 71), 0)
    ia3_scale = jnp.clip(1.0 + 0.18 * jax.random.normal(keys[6], (FF,), jnp.float32), 0.1, 1.9)
    return dict(tokens=tokens, cotangent=cotangent, weight_codes=weight_codes, block_scales=block_scales, block_index=block_index, block_count=block_count, ia3_scale=ia3_scale)


def dequant(codes, scales, live_slots):
    values = codes.astype(jnp.float32) - 8.0
    return (values * scales[..., None, :] * live_slots[..., None, None]).astype(jnp.bfloat16)


def reference(tokens, cotangent, weight_codes, block_scales, block_index, block_count, ia3_scale):
    token_total = tokens.shape[0]
    blocks = D // BLK
    token_cube = tokens.reshape(token_total, blocks, BLK)
    grad_cube = cotangent.reshape(token_total, blocks, BLK)

    def per_block(totals, block_row):
        columns_used = block_index[block_row].astype(jnp.int32)
        live_slots = (jnp.arange(KMAX, dtype=jnp.int32) < block_count[block_row]).astype(jnp.float32)
        packed = weight_codes[block_row]
        w_gate = dequant(packed % 16, block_scales[0, block_row], live_slots).astype(jnp.float32)
        w_up = dequant((packed // 16) % 16, block_scales[1, block_row], live_slots).astype(jnp.float32)
        w_down = dequant((packed // 256) % 16, block_scales[2, block_row], live_slots).astype(jnp.float32)
        token_blocks = jnp.take(token_cube, columns_used, axis=1).astype(jnp.float32)
        grad_blocks = jnp.take(grad_cube, columns_used, axis=1).astype(jnp.float32)
        gate_out = jnp.einsum('tki,kio->to', token_blocks, w_gate)
        up_out = jnp.einsum('tki,kio->to', token_blocks, w_up)
        hidden_grad = jnp.einsum('tkc,koc->to', grad_blocks, w_down)
        sigmoid_gate = jax.nn.sigmoid(gate_out)
        activated = gate_out * sigmoid_gate
        scale_here = lax.dynamic_slice_in_dim(ia3_scale, block_row * BLK, BLK)
        ia3_part = jnp.sum(hidden_grad * activated * up_out, axis=0)
        scaled = hidden_grad * scale_here
        up_grad = (scaled * activated).astype(jnp.bfloat16).astype(jnp.float32)
        gate_grad = (scaled * up_out * sigmoid_gate * (1.0 + gate_out * (1.0 - sigmoid_gate))).astype(jnp.bfloat16).astype(jnp.float32)
        contrib = jnp.einsum('to,kio->tki', gate_grad, w_gate) + jnp.einsum('to,kio->tki', up_grad, w_up)
        totals = totals.at[:, columns_used, :].add(contrib)
        return totals, ia3_part

    start_totals = jnp.zeros((token_total, blocks, BLK), jnp.float32)
    summed, ia3_parts = lax.scan(per_block, start_totals, jnp.arange(HID_BLOCKS, dtype=jnp.int32))
    return summed.reshape(token_total, D).astype(jnp.bfloat16), ia3_parts.reshape(FF)
```

```python
import functools

import jax
import jax.numpy as jnp
from jax import lax
from jax.experimental import pallas as pl
from jax.experimental.pallas import tpu as pltpu
from jax.sharding import PartitionSpec as P

NY, NZ = 4, 8
MB = 1 << 20
F32, BF16 = jnp.float32, jnp.bfloat16
ANY = pl.BlockSpec(memory_space=pl.ANY)
SMEM = pl.BlockSpec(memory_space=pltpu.SMEM)


def dev(y, z, c):
    return ((y % NY) * NZ + z % NZ) * 2 + c


def send(a, dy=0, dz=0, flip=False, signed=False):
    pairs = []
    for y in range(NY):
        for z in range(NZ):
            for c in range(2):
                s = -1 if signed and c else 1
                pairs.append((dev(y, z, c), dev(y + s * dy, z + s * dz, 1 - c if flip else c)))
    return lax.ppermute(a, "mp", pairs)


def swap(a):
    return send(a, flip=True)


def dequant_kernel(index_ref, count_ref, codes_ref, scales_ref, gu_ref, down_ref):
    h = pl.program_id(0)
    gu_ref[...] = jnp.zeros_like(gu_ref)
    down_ref[...] = jnp.zeros_like(down_ref)

    def slot(k, carry):
        n = index_ref[h, k]
        words = codes_ref[0, k]

        def part(p):
            v = ((words >> (4 * p)) & 15).astype(F32) - 8.0
            return (v * scales_ref[p, 0, pl.ds(k, 1), :]).astype(BF16)

        gu_ref[0, n, :, 0:128] = part(0)
        gu_ref[0, n, :, 128:256] = part(1)
        down_ref[0, n] = part(2)
        return carry

    lax.fori_loop(0, count_ref[h], slot, 0)


def dequant(codes, scales, index, count):
    hb, slots = index.shape
    return pl.pallas_call(
        dequant_kernel,
        grid=(hb,),
        in_specs=[
            SMEM,
            SMEM,
            pl.BlockSpec((1, slots, 128, 128), lambda h: (h, 0, 0, 0)),
            pl.BlockSpec((3, 1, slots, 128), lambda h: (0, h, 0, 0)),
        ],
        out_specs=[
            pl.BlockSpec((1, 64, 128, 256), lambda h: (h, 0, 0, 0)),
            pl.BlockSpec((1, 64, 128, 128), lambda h: (h, 0, 0, 0)),
        ],
        out_shape=[
            jax.ShapeDtypeStruct((hb, 64, 128, 256), BF16),
            jax.ShapeDtypeStruct((hb, 64, 128, 128), BF16),
        ],
        compiler_params=pltpu.CompilerParams(vmem_limit_bytes=32 * MB),
        cost_estimate=pl.CostEstimate(flops=60_000_000, bytes_accessed=30 * MB, transcendentals=0),
        name="dequant",
    )(index, count, codes, scales)


def chip_of(pos_ref, dy, dz):
    y, z = pos_ref[0], pos_ref[1]
    return lax.rem(y + dy + 2 * NY, NY) * NZ + lax.rem(z + dz + 2 * NZ, NZ)


def gate_up_kernel(places, pos_ref, w_ref, *refs):
    pieces, (out_ref, tok, sem) = refs[: len(places)], refs[len(places) :]
    h = pl.program_id(0)
    sign = 1 - 2 * pos_ref[2]

    def copies():
        for piece, place in zip(pieces, places):
            for q, (dy, dz) in enumerate(place(sign)):
                j = chip_of(pos_ref, dy, dz)
                yield pltpu.make_async_copy(piece.at[pl.ds(2 * q, 2)], tok.at[pl.ds(2 * j, 2)], sem)

    @pl.when(h == 0)
    def _():
        for cp in copies():
            cp.start()
        for cp in copies():
            cp.wait()

    acc = jnp.zeros((256, 256), F32)
    for g in range(4):
        lhs = jnp.concatenate([tok[16 * g + i] for i in range(16)], axis=1)
        rhs = w_ref[0, 16 * g : 16 * g + 16].reshape(2048, 256)
        acc += jnp.dot(lhs, rhs, preferred_element_type=F32)
    out_ref[0] = acc.T


def gate_up(pos, w, pieces, places):
    hb = w.shape[0]
    return pl.pallas_call(
        functools.partial(gate_up_kernel, places),
        grid=(hb,),
        in_specs=[SMEM, pl.BlockSpec((1, 64, 128, 256), lambda h: (h, 0, 0, 0))] + [ANY] * len(pieces),
        out_specs=pl.BlockSpec((1, 256, 256), lambda h: (h, 0, 0)),
        out_shape=jax.ShapeDtypeStruct((hb, 256, 256), F32),
        scratch_shapes=[pltpu.VMEM((64, 256, 128), BF16), pltpu.SemaphoreType.DMA],
        compiler_params=pltpu.CompilerParams(vmem_limit_bytes=32 * MB),
        cost_estimate=pl.CostEstimate(flops=3_300_000_000, bytes_accessed=17 * MB, transcendentals=0),
        name="gate_up",
    )(pos, w, *pieces)


def hidden_kernel(places, pos_ref, gu_ref, scale_ref, w_ref, *refs):
    pieces = refs[: len(places)]
    grad_ref, ia3_ref, cot, wv, sem, wsem = refs[len(places) :]
    sign = 1 - 2 * pos_ref[2]

    def copies():
        for piece, place in zip(pieces, places):
            for q, (dy, dz) in enumerate(place(sign)):
                j = chip_of(pos_ref, dy, dz)
                yield pltpu.make_async_copy(piece.at[pl.ds(2 * q, 2)], cot.at[pl.ds(2 * j, 2)], sem)

    def wcopy(g):
        cut = pl.ds(16 * g, 16)
        return pltpu.make_async_copy(w_ref.at[:, cut], wv.at[:, cut], wsem.at[g])

    for cp in copies():
        cp.start()
    for g in range(4):
        wcopy(g).start()
    for cp in copies():
        cp.wait()
    acc = jnp.zeros((384, 256), F32)
    for g in range(4):
        wcopy(g).wait()
        lhs = jnp.concatenate(
            [jnp.concatenate([wv[h, 16 * g + i] for i in range(16)], axis=1) for h in range(3)], axis=0
        )
        rhs = cot[16 * g : 16 * g + 16].reshape(2048, 256)
        acc += jnp.dot(lhs, rhs, preferred_element_type=F32)
    for h in range(3):
        hidden = acc[128 * h : 128 * h + 128]
        gate = gu_ref[h, 0:128]
        up = gu_ref[h, 128:256]
        s = jax.nn.sigmoid(gate)
        activated = gate * s
        ia3_ref[128 * h : 128 * h + 128, :] = jnp.sum(hidden * activated * up, axis=1, keepdims=True)
        scaled = hidden * scale_ref[128 * h : 128 * h + 128, :]
        grad_ref[h, 0:128] = (scaled * up * s * (1.0 + gate * (1.0 - s))).astype(BF16)
        grad_ref[h, 128:256] = (scaled * activated).astype(BF16)


def hidden_grads(pos, gu, scale, w, pieces, places):
    hb = w.shape[0]
    vm = pl.BlockSpec(memory_space=pltpu.VMEM)
    return pl.pallas_call(
        functools.partial(hidden_kernel, places),
        in_specs=[SMEM, vm, vm] + [ANY] * (1 + len(pieces)),
        out_specs=[vm, vm],
        out_shape=[
            jax.ShapeDtypeStruct((hb, 256, 256), BF16),
            jax.ShapeDtypeStruct((hb * 128, 1), F32),
        ],
        scratch_shapes=[
            pltpu.VMEM((64, 128, 256), BF16),
            pltpu.VMEM((hb, 64, 128, 128), BF16),
            pltpu.SemaphoreType.DMA,
            pltpu.SemaphoreType.DMA((4,)),
        ],
        compiler_params=pltpu.CompilerParams(vmem_limit_bytes=32 * MB),
        cost_estimate=pl.CostEstimate(flops=1_700_000_000, bytes_accessed=11 * MB, transcendentals=100_000),
        name="hidden",
    )(pos, gu, scale, w, *pieces)


def input_kernel(order, flip, pos_ref, grad_ref, w_ref, out_ref, wv, sem):
    par = 1 - pos_ref[2] if flip else pos_ref[2]
    groups = len(order) // 4
    hb = grad_ref.shape[0]

    def copies(g):
        for i in range(4):
            j = chip_of(pos_ref, *order[4 * g + i])
            yield pltpu.make_async_copy(w_ref.at[:, 2 * j + par], wv.at[:, 4 * g + i], sem.at[g])

    for g in range(groups):
        for cp in copies(g):
            cp.start()
    for g in range(groups):
        for cp in copies(g):
            cp.wait()
        acc = jnp.zeros((512, 256), F32)
        for h in range(hb):
            lhs = wv[h, 4 * g : 4 * g + 4].reshape(512, 256)
            acc += jnp.dot(lhs, grad_ref[h], preferred_element_type=F32)
        out_ref[4 * g : 4 * g + 4] = acc.reshape(4, 128, 256).astype(out_ref.dtype)


def input_part(pos, grad, w, order, flip):
    hb = w.shape[0]
    vm = pl.BlockSpec(memory_space=pltpu.VMEM)
    n = len(order)
    return pl.pallas_call(
        functools.partial(input_kernel, order, flip),
        in_specs=[SMEM, vm, ANY],
        out_specs=vm,
        out_shape=jax.ShapeDtypeStruct((n, 128, 256), BF16),
        scratch_shapes=[pltpu.VMEM((hb, n, 128, 256), BF16), pltpu.SemaphoreType.DMA((n // 4,))],
        compiler_params=pltpu.CompilerParams(vmem_limit_bytes=32 * MB),
        cost_estimate=pl.CostEstimate(
            flops=n * 2 * 128 * 256 * 256 * hb, bytes_accessed=n * 65536 * (hb + 1), transcendentals=0
        ),
        name="input_part",
    )(pos, grad, w)


def on_device(tokens, cotangent, weight_codes, block_scales, block_index, block_count, ia3_scale):
    m = lax.axis_index("mp")
    core = lax.rem(m, 2)
    pos = jnp.stack([m // (2 * NZ), lax.rem(m // 2, NZ), core]).astype(jnp.int32)
    first = core == 0

    def ordered(mine, other):
        return jnp.where(first, mine, other), jnp.where(first, other, mine)

    w_gu, w_down = dequant(weight_codes, block_scales, block_index, block_count)

    with jax.named_scope("gather"):
        own_t = tokens[None]
        own_c = cotangent.T[None]
        sib_t = swap(own_t)
        sib_c = swap(own_c)
        chip_t = jnp.concatenate(ordered(own_t, sib_t), 0)
        y1 = send(chip_t, dy=1, signed=True)
        y2 = send(own_t, dy=2)
        y1s, y2s = swap(y1), swap(y2)
        t0 = jnp.concatenate((chip_t,) + ordered(y2, y2s), 0)
        t1 = jnp.concatenate(ordered(y1, y1s), 0)

        t_pieces, t_places = [t0, t1], [lambda s: ((0, 0), (2, 0)), lambda s: ((-1, 0), (1, 0))]

        def add_t(piece, dys, step):
            t_pieces.append(piece)
            t_places.append(lambda s: tuple((dy(s), step * s) for dy in dys))

        def fixed(v):
            return lambda s: v

        f0, f1 = t0, t1
        for step in (1, 2, 3):
            f0 = send(f0, dz=1, signed=True)
            f1 = send(f1, dz=1, signed=True)
            for f, dys in ((f0, (0, 2)), (f1, (-1, 1))):
                add_t(f, [fixed(v) for v in dys], -step)
                add_t(swap(f), [fixed(v) for v in dys], step)
        f4 = send(jnp.where(first, f0, f1), dz=1, signed=True)
        add_t(f4, [lambda s: (s - 1) // 2, lambda s: 1 + (s + 1) // 2], 4)
        add_t(swap(f4), [lambda s: (-s - 1) // 2, lambda s: 1 + (1 - s) // 2], 4)

        chip_c = jnp.concatenate(ordered(own_c, sib_c), 0)
        q = [send(chip_c, dz=d, signed=True) for d in (1, 2, 3)]
        q4 = send(own_c, dz=4)
        qs = [swap(v) for v in q]
        q4s = swap(q4)
        c0 = jnp.concatenate((chip_c,) + ordered(q4, q4s) + ordered(q[0], qs[0]), 0)
        c1 = jnp.concatenate(ordered(q[1], qs[1]) + ordered(q[2], qs[2]), 0)
        dz0, dz1 = (0, 4, -1, 1), (-2, 2, -3, 3)
        e0 = send(c0, dy=1, signed=True)
        e1 = send(c1, dy=1, signed=True)
        e2 = send(jnp.where(first, e0, e1), dy=1, signed=True)
        c_pieces = [c0, c1, e0, swap(e0), e1, swap(e1), e2, swap(e2)]

        def pick(sel):
            return tuple((2, (1 + sel) // 2 * u + (1 - sel) // 2 * v) for u, v in zip(dz0, dz1))

        c_places = [
            lambda s: tuple((0, d) for d in dz0),
            lambda s: tuple((0, d) for d in dz1),
            lambda s: tuple((-s, d) for d in dz0),
            lambda s: tuple((s, d) for d in dz0),
            lambda s: tuple((-s, d) for d in dz1),
            lambda s: tuple((s, d) for d in dz1),
            lambda s: pick(s),
            lambda s: pick(-s),
        ]

    gu = gate_up(pos, w_gu, t_pieces, t_places)
    grad, ia3_part = hidden_grads(pos, gu, ia3_scale[:, None], w_down, c_pieces, c_places)

    with jax.named_scope("ia3"):
        ia3_part = ia3_part[:, 0]
        size = lax.axis_size("dp")
        p1, p2, p3 = (lax.ppermute(ia3_part, "dp", [(i, i ^ k) for i in range(size)]) for k in (1, 2, 3))
        ia3_grad = (ia3_part + p1) + (p2 + p3)

    with jax.named_scope("scatter"):
        kept = []
        arrived = []
        for dzs in ((4, 3, 5, 2), (6, 1, 7, 0)):
            order = [(dy, dz) for dy in (2, 1, 3, 0) for dz in dzs]
            away = input_part(pos, grad, w_gu, order, True)
            here = input_part(pos, grad, w_gu, order, False)
            total = swap(away).astype(F32) + here.astype(F32)
            parts = [total[4 * i : 4 * i + 4].astype(BF16) for i in range(3)]
            got = [send(p, dy=dy) for p, dy in zip(parts, (2, 1, 3))]
            mine = total[12:16] + got[0].astype(F32) + got[1].astype(F32) + got[2].astype(F32)
            for i, dz in enumerate(dzs):
                if dz:
                    arrived.append(send(mine[i].astype(BF16), dz=dz))
                else:
                    kept = mine[i]
        out = kept
        for a in arrived:
            out = out + a.astype(F32)
        input_grad = out.T.astype(BF16)
    return (input_grad, ia3_grad)


def solution(mesh):
    return jax.shard_map(
        on_device,
        mesh=mesh,
        in_specs=(
            P("dp", "mp"),
            P("dp", "mp"),
            P("mp", None, None, None),
            P(None, "mp", None, None),
            P("mp", None),
            P("mp"),
            P("mp"),
        ),
        out_specs=(P("dp", "mp"), P("mp")),
        check_vma=False,
    )
```

```python
import functools

import jax
import jax.numpy as jnp
from jax import lax
from jax.experimental import pallas as pl
from jax.experimental.pallas import tpu as pltpu
from jax.sharding import PartitionSpec as P

NY, NZ = 4, 8
MB = 1 << 20
F32, BF16 = jnp.float32, jnp.bfloat16
VMEM = pl.BlockSpec(memory_space=pltpu.VMEM)
ANY = pl.BlockSpec(memory_space=pl.ANY)
SMEM = pl.BlockSpec(memory_space=pltpu.SMEM)


def dev(y, z, c):
    return ((y % NY) * NZ + z % NZ) * 2 + c


def send(a, dy=0, dz=0, flip=False, signed=False):
    pairs = []
    for y in range(NY):
        for z in range(NZ):
            for c in range(2):
                s = -1 if signed and c else 1
                pairs.append((dev(y, z, c), dev(y + s * dy, z + s * dz, 1 - c if flip else c)))
    return lax.ppermute(a, "mp", pairs)


def swap(a):
    return send(a, flip=True)


def array(shape, dtype):
    return jax.ShapeDtypeStruct(shape, dtype)


FLAG = array((1,), jnp.int32)


def call(kernel, name, ins, outs, scratch=(), limit=6, flops=0, after=(), keep=()):
    def space(a):
        return SMEM if a.dtype == jnp.int32 and a.size < 1024 else VMEM

    skip = len(after) + len(keep)
    size = sum(a.size * a.dtype.itemsize for a in tuple(ins) + tuple(outs))
    return pl.pallas_call(
        (lambda *refs: kernel(*refs[skip:])) if skip else kernel,
        in_specs=[ANY] * len(after) + [VMEM] * len(keep) + [space(a) for a in ins],
        out_specs=[space(a) for a in outs],
        out_shape=list(outs),
        scratch_shapes=list(scratch),
        compiler_params=pltpu.CompilerParams(vmem_limit_bytes=limit * MB),
        cost_estimate=pl.CostEstimate(flops=flops, bytes_accessed=size, transcendentals=0),
        name=name,
    )(*after, *keep, *ins)


CHUNK = 16


def dequant_kernel(h, codes_ref, index_ref, count_ref, scales_ref, gu_ref, down_ref, flag_ref, words, sems):
    flag_ref[0] = 0
    count = count_ref[h]
    cuts = range(0, 48, CHUNK)

    def copy(kc):
        b = kc // CHUNK
        return pltpu.make_async_copy(codes_ref.at[h, pl.ds(kc, CHUNK)], words.at[b], sems.at[b])

    for kc in cuts:
        copy(kc).start()
    gu_ref[...] = jnp.zeros(gu_ref.shape, BF16)
    down_ref[...] = jnp.zeros(down_ref.shape, BF16)
    for kc in cuts:
        copy(kc).wait()

        def slots(s, carry):
            for u in range(4):
                j = 4 * s + u
                k = kc + j
                n = index_ref[h, k]
                live = jnp.where(k < count, 1.0, 0.0).astype(F32)
                coded = words[kc // CHUNK, j] ^ 0x888

                def part(p):
                    v = ((coded << (28 - 4 * p)) >> 28).astype(F32)
                    return (v * (scales_ref[p, h, pl.ds(k, 1), :] * live)).astype(BF16)

                gu_ref[n, :, 0:128] = part(0)
                gu_ref[n, :, 128:256] = part(1)
                down_ref[n] = part(2)
            return carry

        lax.fori_loop(0, jnp.clip((count - kc + 3) // 4, 0, CHUNK // 4), slots, 0)


def dequant(h, codes, scales, index, count, after=()):
    outs = (array((64, 128, 256), BF16), array((64, 128, 128), BF16), FLAG)
    kernel = functools.partial(dequant_kernel, h)
    skip = len(after)
    return pl.pallas_call(
        (lambda *refs: kernel(*refs[skip:])) if skip else kernel,
        in_specs=[ANY] * skip + [ANY, SMEM, SMEM, VMEM],
        out_specs=[VMEM, VMEM, SMEM],
        out_shape=outs,
        scratch_shapes=[pltpu.VMEM((48 // CHUNK, CHUNK, 128, 128), jnp.int32), pltpu.SemaphoreType.DMA((48 // CHUNK,))],
        compiler_params=pltpu.CompilerParams(vmem_limit_bytes=14 * MB),
        cost_estimate=pl.CostEstimate(flops=12_000_000, bytes_accessed=10 * MB, transcendentals=0),
        name="dequant",
    )(*after, codes, index, count, scales)


def chip_of(pos_ref, dy, dz):
    y, z = pos_ref[0], pos_ref[1]
    return lax.rem(y + dy + 2 * NY, NY) * NZ + lax.rem(z + dz + 2 * NZ, NZ)


def chips(pos_ref, places):
    sign = 1 - 2 * pos_ref[2]
    return [chip_of(pos_ref, dy, dz) for place in places for dy, dz in place(sign)]


def own_kernel(tok, cot, sib_t, sib_c, pos_ref, chip_t, chip_c, own_c, tv, cv, sems):
    c = pos_ref[2]
    moves = (
        pltpu.make_async_copy(cot, cv.at[0], sems.at[0]),
        pltpu.make_async_copy(sib_c, cv.at[1], sems.at[1]),
        pltpu.make_async_copy(tok, tv.at[0], sems.at[2]),
        pltpu.make_async_copy(sib_t, tv.at[1], sems.at[3]),
    )
    for move in moves:
        move.start()
    moves[0].wait()
    mine = cv[0].T
    own_c[...] = mine
    chip_c[c] = mine
    moves[1].wait()
    chip_c[1 - c] = cv[1].T
    moves[2].wait()
    chip_t[c] = tv[0]
    moves[3].wait()
    chip_t[1 - c] = tv[1]


def own(pos, tokens, cotangent, sib_t, sib_c):
    return pl.pallas_call(
        own_kernel,
        in_specs=[ANY] * 4 + [SMEM],
        out_specs=[VMEM] * 3,
        out_shape=[array((2, 256, 128), BF16), array((2, 128, 256), BF16), array((128, 256), BF16)],
        scratch_shapes=[
            pltpu.VMEM((2, 256, 128), BF16),
            pltpu.VMEM((2, 256, 128), BF16),
            pltpu.SemaphoreType.DMA((4,)),
        ],
        compiler_params=pltpu.CompilerParams(vmem_limit_bytes=6 * MB),
        cost_estimate=pl.CostEstimate(flops=0, bytes_accessed=MB, transcendentals=0),
        name="own",
    )(tokens, cotangent, sib_t, sib_c, pos)


def stack_kernel(*refs):
    out, at = refs[-1], 0
    for r in refs[:-1]:
        n = r.shape[0] if len(r.shape) == 3 else 1
        out[at : at + n] = r[...].reshape((n,) + r.shape[-2:])
        at += n


def stack(parts, after=()):
    n = sum(p.shape[0] if p.ndim == 3 else 1 for p in parts)
    return call(stack_kernel, "stack", tuple(parts), (array((n,) + parts[0].shape[-2:], BF16),), after=after)[0]


def merge_t_kernel(pos_ref, chip, mine, other, t0, t1):
    c = pos_ref[2]
    t0[0:2] = chip[...]
    t0[2 + c] = mine[2]
    t0[3 - c] = other[2]
    t1[pl.ds(2 * c, 2)] = mine[0:2]
    t1[pl.ds(2 - 2 * c, 2)] = other[0:2]


def merge_c_kernel(pos_ref, chip, mine, other, out):
    c = pos_ref[2]
    out[0:2] = chip[...]
    out[2 + c] = mine[6]
    out[3 - c] = other[6]
    for i in range(3):
        out[pl.ds(4 + 4 * i + 2 * c, 2)] = mine[2 * i : 2 * i + 2]
        out[pl.ds(6 + 4 * i - 2 * c, 2)] = other[2 * i : 2 * i + 2]


def part_kernel(pos_ref, a, out):
    n = out.shape[0]
    out[...] = a[pl.ds(n * pos_ref[2], n)]


def part_of(pos, a, after):
    return call(part_kernel, "part", (pos, a), (array((a.shape[0] // 2,) + a.shape[1:], a.dtype),), after=after, flops=15_000_000_000)[0]


def pick_kernel(pos_ref, a, b, out):
    @pl.when(pos_ref[2] == 0)
    def _():
        out[...] = a[...]

    @pl.when(pos_ref[2] == 1)
    def _():
        out[...] = b[...]


def pick(pos, a, b, after=(), keep=()):
    return call(pick_kernel, "pick", (pos, a, b), (array(a.shape, a.dtype),), after=after, keep=keep)[0]


def gate_up_kernel(places, first, last, pos_ref, w0, w1, w2, *refs):
    pieces = refs[: len(places)]
    rest = refs[len(places) :]
    out_ref, flag_ref = rest[-2], rest[-1]
    flag_ref[0] = 0
    where = chips(pos_ref, places)
    blocks = [piece[i] for piece in pieces for i in range(piece.shape[0])]
    for h, w in enumerate((w0, w1, w2)):
        acc = None if first else rest[0][h]
        for g in range(0, len(where), 8):
            cut = where[g : g + 8]
            lhs = jnp.concatenate(blocks[2 * g : 2 * g + 2 * len(cut)], axis=1)
            rhs = jnp.concatenate([w[pl.ds(2 * j, 2)].reshape(256, 256) for j in cut], axis=0)
            term = jnp.dot(lhs, rhs, preferred_element_type=F32)
            acc = term if acc is None else acc + term
        out_ref[h] = acc.T if last else acc


def gate_up(pos, ws, pieces, places, acc=None, last=False, after=()):
    ins = (pos,) + tuple(ws) + tuple(pieces) + (() if acc is None else (acc,))
    return call(
        functools.partial(gate_up_kernel, places, acc is None, last),
        "gate_up",
        ins,
        (array((3, 256, 256), F32), FLAG),
        limit=24,
        flops=sum(p.shape[0] for p in pieces) * 2 * 256 * 128 * 768,
        after=after,
    )


def hidden_kernel(places, first, last, pos_ref, w0, w1, w2, *refs):
    pieces = refs[: len(places)]
    rest = refs[len(places) :]
    where = chips(pos_ref, places)
    blocks = [piece[i] for piece in pieces for i in range(piece.shape[0])]
    acc = None if first else rest[0][...]
    for g in range(0, len(where), 8):
        cut = where[g : g + 8]
        lhs = jnp.concatenate(
            [jnp.concatenate([w[2 * j + c] for j in cut for c in range(2)], axis=1) for w in (w0, w1, w2)],
            axis=0,
        )
        rhs = jnp.concatenate([blocks[2 * i + c] for i in range(g, g + 8) for c in range(2)], axis=0)
        term = jnp.dot(lhs, rhs, preferred_element_type=F32)
        acc = term if acc is None else acc + term
    if not last:
        rest[-1][...] = acc
        return
    gu_ref, scale_ref, grad_ref, ia3_ref = rest[-4:]
    for h in range(3):
        rows = slice(128 * h, 128 * h + 128)
        hidden = acc[rows]
        gate = gu_ref[h, 0:128]
        up = gu_ref[h, 128:256]
        s = jax.nn.sigmoid(gate)
        activated = gate * s
        ia3_ref[:, rows] = jnp.sum((hidden * activated * up).T, axis=0, keepdims=True)
        scaled = hidden * scale_ref[rows, :]
        grad_ref[h, 0:128] = (scaled * up * s * (1.0 + gate * (1.0 - s))).astype(BF16)
        grad_ref[h, 128:256] = (scaled * activated).astype(BF16)


def hidden(pos, ws, pieces, places, acc=None, gu=None, scale=None):
    last = gu is not None
    ins = (pos,) + tuple(ws) + tuple(pieces) + (() if acc is None else (acc,)) + ((gu, scale) if last else ())
    outs = (array((3, 256, 256), BF16), array((1, 384), F32)) if last else (array((384, 256), F32),)
    return call(
        functools.partial(hidden_kernel, places, acc is None, last),
        "hidden",
        ins,
        outs,
        limit=16,
        flops=sum(p.shape[0] for p in pieces) * 2 * 384 * 128 * 256,
    )


def input_kernel(order, par_of, pos_ref, grad_ref, w0, w1, w2, *refs):
    par = par_of(pos_ref[2])
    where = [2 * chip_of(pos_ref, dy, dz) + par for dy, dz in order]
    added, outs = (refs[0], refs[1:]) if len(refs) > 1 else (None, refs)
    for g in range(0, len(order), 4):
        cut = where[g : g + 4]
        acc = None
        for h, w in enumerate((w0, w1, w2)):
            lhs = jnp.concatenate([w[j] for j in cut], axis=0)
            term = jnp.dot(lhs, grad_ref[h], preferred_element_type=F32)
            acc = term if acc is None else acc + term
        acc = acc.reshape(len(cut), 128, 256)
        if added is not None:
            acc = acc + added[g : g + 4].astype(F32)
            outs[g // 4][...] = acc.astype(outs[g // 4].dtype)
        else:
            outs[0][g : g + 4] = acc.astype(BF16)


def input_part(pos, grad, ws, order, added=None, after=()):
    n = len(order)
    if added is None:
        kernel = functools.partial(input_kernel, order, lambda c: 1 - c)
        outs = [array((n, 128, 256), BF16)]
    else:
        kernel = functools.partial(input_kernel, order, lambda c: c)
        outs = [array((4, 128, 256), BF16)] * (n // 4 - 2) + [array((4, 128, 256), F32)] * 2
    return call(
        kernel,
        "input_away" if added is None else "input_here",
        (pos, grad) + tuple(ws) + (() if added is None else (added,)),
        outs,
        limit=24,
        flops=n * 2 * 128 * 256 * 768,
        after=after,
    )


def add_kernel(a, r, out):
    out[...] = (a[...] + r[...].astype(F32)).astype(BF16)


def add(a, r):
    return call(add_kernel, "add", (a, r), (array(a.shape, BF16),))[0]


def y_sum_kernel(pos_ref, a0, ra1, ra3, b0, rb1, rb3, out):
    for i in range(4):
        for at, v, r, q in ((i, a0, ra1, ra3), (i + 4, b0, rb1, rb3)):
            total = v[i] + (r[i].astype(F32) + q[i].astype(F32))
            out[lax.rem(pos_ref[1] + at, NZ)] = total.astype(BF16)


def z_sum_kernel(parts, out):
    v = parts[0].astype(F32)
    for i in range(1, NZ):
        v = v + parts[i].astype(F32)
    out[...] = v.T.astype(BF16)


def on_device(tokens, cotangent, weight_codes, block_scales, block_index, block_count, ia3_scale):
    m = lax.axis_index("mp")
    pos = jnp.stack([m // (2 * NZ), lax.rem(m // 2, NZ), lax.rem(m, 2)]).astype(jnp.int32)
    block = (256, 128)

    with jax.named_scope("gather"):
        sib_t = swap(tokens)
        sib_c = swap(cotangent)
        chip_t, chip_c, own_c = own(pos, tokens, cotangent, sib_t, sib_c)
        near_t = stack([send(chip_t, dy=1, signed=True), send(tokens, dy=2)])
        t0, t1 = call(merge_t_kernel, "merge_t", (pos, chip_t, near_t, swap(near_t)), [array((4, 256, 128), BF16)] * 2)
        near_c = stack([send(chip_c, dz=d, signed=True) for d in (1, 2, 3)] + [send(own_c, dz=4)], after=(near_t,))
        c0 = call(
            merge_c_kernel, "merge_c", (pos, chip_c, near_c, swap(near_c)), [array((16, 128, 256), BF16)]
        )[0]
        e1 = send(c0, dy=1, signed=True)
        ws = [dequant(h, weight_codes, block_scales, block_index, block_count, (c0,)) for h in range(3)]
        w_gu, w_down, ready = ([w[i] for w in ws] for i in range(3))

        f0, f1, steps = t0, t1, []
        for i in range(3):
            if i:
                f1, ready[i - 1] = lax.optimization_barrier((f1, ready[i - 1]))
            f0 = send(f0, dz=1, signed=True)
            f1 = send(f1, dz=1, signed=True)
            steps.append((f0, f1))
        mine = stack(steps[0] + steps[1])
        ys = (0, 2, -1, 1)
        t_pieces = [t0, t1, mine, swap(mine)]
        t_places = [
            lambda s: ((0, 0), (2, 0)),
            lambda s: ((-1, 0), (1, 0)),
            lambda s: tuple((dy, -n * s) for n in (1, 2) for dy in ys),
            lambda s: tuple((dy, n * s) for n in (1, 2) for dy in ys),
        ]
        gu, _ = gate_up(pos, w_gu, t_pieces, t_places, after=tuple(ready))
        e2 = send(part_of(pos, e1, ()), dy=1, signed=True)
        c_pieces = [c0, e1, swap(e1), e2, swap(e2)]
        dzs = (0, 4, -1, 1, -2, 2, -3, 3)

        def chosen(sel):
            return tuple((2, (1 + sel) // 2 * u + (1 - sel) // 2 * v) for u, v in zip(dzs[:4], dzs[4:]))

        c_places = [
            lambda s: tuple((0, d) for d in dzs),
            lambda s: tuple((-s, d) for d in dzs),
            lambda s: tuple((s, d) for d in dzs),
            lambda s: chosen(s),
            lambda s: chosen(-s),
        ]
        (part,) = hidden(pos, w_down, c_pieces[:3], c_places[:3])
        f4 = send(pick(pos, f0, f1, after=(ready[2],)), dz=1, signed=True)
        f4, gu, part = lax.optimization_barrier((f4, gu, part))
        mine = stack(steps[2])
        t_pieces = [mine, swap(mine), f4, swap(f4)]
        t_places = [
            lambda s: tuple((dy, -3 * s) for dy in ys),
            lambda s: tuple((dy, 3 * s) for dy in ys),
            lambda s: (((s - 1) // 2, 4), (1 + (s + 1) // 2, 4)),
            lambda s: (((-s - 1) // 2, 4), (1 + (1 - s) // 2, 4)),
        ]
        gu, _ = gate_up(pos, w_gu, t_pieces, t_places, gu, last=True)

        grad, ia3_part = hidden(pos, w_down, c_pieces[3:], c_places[3:], part, gu, ia3_scale[:, None])

    with jax.named_scope("ia3"):
        ia3_part = ia3_part.reshape(384)
        ia3_part = ia3_part + lax.ppermute(ia3_part, "dp", [(0, 1), (1, 0), (2, 3), (3, 2)])
        ia3_grad = ia3_part + lax.ppermute(ia3_part, "dp", [(0, 3), (3, 0), (1, 2), (2, 1)])

    with jax.named_scope("scatter"):
        cuts = ((0, 1, 2, 3), (4, 5, 6, 7))
        ways = ((2, 3, 1, 0), (2, 1, 3, 0))
        orders = [[(dy, dz) for dy in way for dz in dzs] for way, dzs in zip(ways, cuts)]
        sib = [swap(input_part(pos, grad, w_gu, order)[0]) for order in orders]
        a2, a3, a1, a0 = input_part(pos, grad, w_gu, orders[0], sib[0])
        ra2 = send(a2, dy=1)
        ra3 = send(a3, dy=-1)
        b2, b1, b3, b0 = input_part(pos, grad, w_gu, orders[1], sib[1])
        rb2 = send(b2, dy=-1)
        rb1 = send(b1, dy=1)
        ra1 = send(add(a1, ra2), dy=1)
        rb3 = send(add(b3, rb2), dy=-1)
        ra1, ia3_grad = lax.optimization_barrier((ra1, ia3_grad))
        total = call(y_sum_kernel, "y_sum", (pos, a0, ra1, ra3, b0, rb1, rb3), [array((8, 128, 256), BF16)])[0]
        columns = [[dev(y, z, c) for z in range(NZ)] for y in range(NY) for c in range(2)]
        total = lax.all_to_all(total, "mp", 0, 0, axis_index_groups=columns, tiled=True)
        input_grad = call(z_sum_kernel, "z_sum", (total,), [array((256, 128), BF16)])[0]
    return (input_grad, ia3_grad)


def solution(mesh):
    return jax.shard_map(
        on_device,
        mesh=mesh,
        in_specs=(
            P("dp", "mp"),
            P("dp", "mp"),
            P("mp", None, None, None),
            P(None, "mp", None, None),
            P("mp", None),
            P("mp"),
            P("mp"),
        ),
        out_specs=(P("dp", "mp"), P("mp")),
        check_vma=False,
    )
```

```python
import functools

import jax
import jax.numpy as jnp
from jax import lax
from jax.experimental import pallas as pl
from jax.experimental.pallas import tpu as pltpu
from jax.sharding import PartitionSpec as P

NY, NZ = 4, 8
MB = 1 << 20
F32, BF16 = jnp.float32, jnp.bfloat16
VMEM = pl.BlockSpec(memory_space=pltpu.VMEM)
ANY = pl.BlockSpec(memory_space=pl.ANY)
SMEM = pl.BlockSpec(memory_space=pltpu.SMEM)


def dev(y, z, c):
    return ((y % NY) * NZ + z % NZ) * 2 + c


def send(a, dy=0, dz=0, flip=False, signed=False):
    pairs = []
    for y in range(NY):
        for z in range(NZ):
            for c in range(2):
                s = -1 if signed and c else 1
                pairs.append((dev(y, z, c), dev(y + s * dy, z + s * dz, 1 - c if flip else c)))
    return lax.ppermute(a, "mp", pairs)


def swap(a):
    return send(a, flip=True)


def array(shape, dtype):
    return jax.ShapeDtypeStruct(shape, dtype)


FLAG = array((1,), jnp.int32)


def call(kernel, name, ins, outs, scratch=(), limit=6, flops=0, after=(), keep=()):
    def space(a):
        return SMEM if a.dtype == jnp.int32 and a.size < 1024 else VMEM

    skip = len(after) + len(keep)
    size = sum(a.size * a.dtype.itemsize for a in tuple(ins) + tuple(outs))
    return pl.pallas_call(
        (lambda *refs: kernel(*refs[skip:])) if skip else kernel,
        in_specs=[ANY] * len(after) + [VMEM] * len(keep) + [space(a) for a in ins],
        out_specs=[space(a) for a in outs],
        out_shape=list(outs),
        scratch_shapes=list(scratch),
        compiler_params=pltpu.CompilerParams(vmem_limit_bytes=limit * MB),
        cost_estimate=pl.CostEstimate(flops=flops, bytes_accessed=size, transcendentals=0),
        name=name,
    )(*after, *keep, *ins)


CHUNK = 16


def dequant_kernel(h, codes_ref, index_ref, count_ref, scales_ref, gu_ref, down_ref, flag_ref, words, sems):
    flag_ref[0] = 0
    count = count_ref[h]
    cuts = range(0, 48, CHUNK)

    def copy(kc):
        b = kc // CHUNK
        return pltpu.make_async_copy(codes_ref.at[h, pl.ds(kc, CHUNK)], words.at[b], sems.at[b])

    for kc in cuts:
        copy(kc).start()
    gu_ref[...] = jnp.zeros(gu_ref.shape, BF16)
    down_ref[...] = jnp.zeros(down_ref.shape, BF16)
    for kc in cuts:
        copy(kc).wait()

        def slots(s, carry):
            for u in range(4):
                j = 4 * s + u
                k = kc + j
                n = index_ref[h, k]
                live = jnp.where(k < count, 1.0, 0.0).astype(F32)
                coded = words[kc // CHUNK, j] ^ 0x888

                def part(p):
                    v = ((coded << (28 - 4 * p)) >> 28).astype(F32)
                    return (v * (scales_ref[p, h, pl.ds(k, 1), :] * live)).astype(BF16)

                gu_ref[n, :, 0:128] = part(0)
                gu_ref[n, :, 128:256] = part(1)
                down_ref[n] = part(2)
            return carry

        lax.fori_loop(0, jnp.clip((count - kc + 3) // 4, 0, CHUNK // 4), slots, 0)


def dequant(h, codes, scales, index, count, after=()):
    outs = (array((64, 128, 256), BF16), array((64, 128, 128), BF16), FLAG)
    kernel = functools.partial(dequant_kernel, h)
    skip = len(after)
    return pl.pallas_call(
        (lambda *refs: kernel(*refs[skip:])) if skip else kernel,
        in_specs=[ANY] * skip + [ANY, SMEM, SMEM, VMEM],
        out_specs=[VMEM, VMEM, SMEM],
        out_shape=outs,
        scratch_shapes=[pltpu.VMEM((48 // CHUNK, CHUNK, 128, 128), jnp.int32), pltpu.SemaphoreType.DMA((48 // CHUNK,))],
        compiler_params=pltpu.CompilerParams(vmem_limit_bytes=14 * MB),
        cost_estimate=pl.CostEstimate(flops=12_000_000, bytes_accessed=10 * MB, transcendentals=0),
        name="dequant",
    )(*after, codes, index, count, scales)


def chip_of(pos_ref, dy, dz):
    y, z = pos_ref[0], pos_ref[1]
    return lax.rem(y + dy + 2 * NY, NY) * NZ + lax.rem(z + dz + 2 * NZ, NZ)


def chips(pos_ref, places):
    sign = 1 - 2 * pos_ref[2]
    return [chip_of(pos_ref, dy, dz) for place in places for dy, dz in place(sign)]


def own_kernel(tok, cot, sib_t, sib_c, pos_ref, chip_t, chip_c, own_c, tv, cv, sems):
    c = pos_ref[2]
    moves = (
        pltpu.make_async_copy(cot, cv.at[0], sems.at[0]),
        pltpu.make_async_copy(sib_c, cv.at[1], sems.at[1]),
        pltpu.make_async_copy(tok, tv.at[0], sems.at[2]),
        pltpu.make_async_copy(sib_t, tv.at[1], sems.at[3]),
    )
    for move in moves:
        move.start()
    moves[0].wait()
    mine = cv[0].T
    own_c[...] = mine
    chip_c[c] = mine
    moves[1].wait()
    chip_c[1 - c] = cv[1].T
    moves[2].wait()
    chip_t[c] = tv[0]
    moves[3].wait()
    chip_t[1 - c] = tv[1]


def own(pos, tokens, cotangent, sib_t, sib_c):
    return pl.pallas_call(
        own_kernel,
        in_specs=[ANY] * 4 + [SMEM],
        out_specs=[VMEM] * 3,
        out_shape=[array((2, 256, 128), BF16), array((2, 128, 256), BF16), array((128, 256), BF16)],
        scratch_shapes=[
            pltpu.VMEM((2, 256, 128), BF16),
            pltpu.VMEM((2, 256, 128), BF16),
            pltpu.SemaphoreType.DMA((4,)),
        ],
        compiler_params=pltpu.CompilerParams(vmem_limit_bytes=6 * MB),
        cost_estimate=pl.CostEstimate(flops=0, bytes_accessed=MB, transcendentals=0),
        name="own",
    )(tokens, cotangent, sib_t, sib_c, pos)


def stack_kernel(*refs):
    out, at = refs[-1], 0
    for r in refs[:-1]:
        n = r.shape[0] if len(r.shape) == 3 else 1
        out[at : at + n] = r[...].reshape((n,) + r.shape[-2:])
        at += n


def stack(parts, after=()):
    n = sum(p.shape[0] if p.ndim == 3 else 1 for p in parts)
    return call(stack_kernel, "stack", tuple(parts), (array((n,) + parts[0].shape[-2:], BF16),), after=after)[0]


def merge_t_kernel(pos_ref, chip, mine, other, t0, t1):
    c = pos_ref[2]
    t0[0:2] = chip[...]
    t0[2 + c] = mine[2]
    t0[3 - c] = other[2]
    t1[pl.ds(2 * c, 2)] = mine[0:2]
    t1[pl.ds(2 - 2 * c, 2)] = other[0:2]


def merge_c_kernel(pos_ref, chip, mine, other, out):
    c = pos_ref[2]
    out[0:2] = chip[...]
    out[2 + c] = mine[6]
    out[3 - c] = other[6]
    for i in range(3):
        out[pl.ds(4 + 4 * i + 2 * c, 2)] = mine[2 * i : 2 * i + 2]
        out[pl.ds(6 + 4 * i - 2 * c, 2)] = other[2 * i : 2 * i + 2]


def part_kernel(pos_ref, a, out):
    n = out.shape[0]
    out[...] = a[pl.ds(n * pos_ref[2], n)]


def part_of(pos, a, after):
    return call(part_kernel, "part", (pos, a), (array((a.shape[0] // 2,) + a.shape[1:], a.dtype),), after=after, flops=15_000_000_000)[0]


def pick_kernel(pos_ref, a, b, out):
    @pl.when(pos_ref[2] == 0)
    def _():
        out[...] = a[...]

    @pl.when(pos_ref[2] == 1)
    def _():
        out[...] = b[...]


def pick(pos, a, b, after=(), keep=()):
    return call(pick_kernel, "pick", (pos, a, b), (array(a.shape, a.dtype),), after=after, keep=keep)[0]


def gate_up_kernel(places, first, last, pos_ref, w0, w1, w2, *refs):
    pieces = refs[: len(places)]
    rest = refs[len(places) :]
    out_ref, flag_ref = rest[-2], rest[-1]
    flag_ref[0] = 0
    where = chips(pos_ref, places)
    blocks = [piece[i] for piece in pieces for i in range(piece.shape[0])]
    for h, w in enumerate((w0, w1, w2)):
        acc = None if first else rest[0][h]
        for g in range(0, len(where), 8):
            cut = where[g : g + 8]
            lhs = jnp.concatenate(blocks[2 * g : 2 * g + 2 * len(cut)], axis=1)
            rhs = jnp.concatenate([w[pl.ds(2 * j, 2)].reshape(256, 256) for j in cut], axis=0)
            term = jnp.dot(lhs, rhs, preferred_element_type=F32)
            acc = term if acc is None else acc + term
        out_ref[h] = acc.T if last else acc


def gate_up(pos, ws, pieces, places, acc=None, last=False, after=()):
    ins = (pos,) + tuple(ws) + tuple(pieces) + (() if acc is None else (acc,))
    return call(
        functools.partial(gate_up_kernel, places, acc is None, last),
        "gate_up",
        ins,
        (array((3, 256, 256), F32), FLAG),
        limit=24,
        flops=sum(p.shape[0] for p in pieces) * 2 * 256 * 128 * 768,
        after=after,
    )


def hidden_kernel(places, first, last, pos_ref, w0, w1, w2, *refs):
    pieces = refs[: len(places)]
    rest = refs[len(places) :]
    where = chips(pos_ref, places)
    blocks = [piece[i] for piece in pieces for i in range(piece.shape[0])]
    acc = None if first else rest[0][...]
    for g in range(0, len(where), 8):
        cut = where[g : g + 8]
        lhs = jnp.concatenate(
            [jnp.concatenate([w[2 * j + c] for j in cut for c in range(2)], axis=1) for w in (w0, w1, w2)],
            axis=0,
        )
        rhs = jnp.concatenate([blocks[2 * i + c] for i in range(g, g + 8) for c in range(2)], axis=0)
        term = jnp.dot(lhs, rhs, preferred_element_type=F32)
        acc = term if acc is None else acc + term
    if not last:
        rest[-1][...] = acc
        return
    gu_ref, scale_ref, grad_ref, ia3_ref = rest[-4:]
    for h in range(3):
        rows = slice(128 * h, 128 * h + 128)
        hidden = acc[rows]
        gate = gu_ref[h, 0:128]
        up = gu_ref[h, 128:256]
        s = jax.nn.sigmoid(gate)
        activated = gate * s
        ia3_ref[:, rows] = jnp.sum((hidden * activated * up).T, axis=0, keepdims=True)
        scaled = hidden * scale_ref[rows, :]
        grad_ref[h, 0:128] = (scaled * up * s * (1.0 + gate * (1.0 - s))).astype(BF16)
        grad_ref[h, 128:256] = (scaled * activated).astype(BF16)


def hidden(pos, ws, pieces, places, acc=None, gu=None, scale=None):
    last = gu is not None
    ins = (pos,) + tuple(ws) + tuple(pieces) + (() if acc is None else (acc,)) + ((gu, scale) if last else ())
    outs = (array((3, 256, 256), BF16), array((1, 384), F32)) if last else (array((384, 256), F32),)
    return call(
        functools.partial(hidden_kernel, places, acc is None, last),
        "hidden",
        ins,
        outs,
        limit=16,
        flops=sum(p.shape[0] for p in pieces) * 2 * 384 * 128 * 256,
    )


def input_kernel(order, par_of, pos_ref, grad_ref, w0, w1, w2, *refs):
    par = par_of(pos_ref[2])
    where = [2 * chip_of(pos_ref, dy, dz) + par for dy, dz in order]
    added, outs = (refs[0], refs[1:]) if len(refs) > 1 else (None, refs)
    for g in range(0, len(order), 4):
        cut = where[g : g + 4]
        acc = None
        for h, w in enumerate((w0, w1, w2)):
            lhs = jnp.concatenate([w[j] for j in cut], axis=0)
            term = jnp.dot(lhs, grad_ref[h], preferred_element_type=F32)
            acc = term if acc is None else acc + term
        acc = acc.reshape(len(cut), 128, 256)
        if added is not None:
            acc = acc + added[g : g + 4].astype(F32)
            outs[g // 4][...] = acc.astype(outs[g // 4].dtype)
        else:
            outs[0][g : g + 4] = acc.astype(BF16)


def input_part(pos, grad, ws, order, added=None, after=()):
    n = len(order)
    if added is None:
        kernel = functools.partial(input_kernel, order, lambda c: 1 - c)
        outs = [array((n, 128, 256), BF16)]
    else:
        kernel = functools.partial(input_kernel, order, lambda c: c)
        outs = [array((4, 128, 256), BF16)] * (n // 4 - 2) + [array((4, 128, 256), F32)] * 2
    return call(
        kernel,
        "input_away" if added is None else "input_here",
        (pos, grad) + tuple(ws) + (() if added is None else (added,)),
        outs,
        limit=24,
        flops=n * 2 * 128 * 256 * 768,
        after=after,
    )


def add_kernel(a, r, out):
    out[...] = (a[...] + r[...].astype(F32)).astype(BF16)


def add(a, r):
    return call(add_kernel, "add", (a, r), (array(a.shape, BF16),))[0]


def y_sum_kernel(pos_ref, a0, ra1, ra3, b0, rb1, rb3, out):
    for i in range(4):
        for at, v, r, q in ((i, a0, ra1, ra3), (i + 4, b0, rb1, rb3)):
            total = v[i] + (r[i].astype(F32) + q[i].astype(F32))
            out[lax.rem(pos_ref[1] + at, NZ)] = total.astype(BF16)


def z_sum_kernel(parts, out):
    v = parts[0].astype(F32)
    for i in range(1, NZ):
        v = v + parts[i].astype(F32)
    out[...] = v.T.astype(BF16)


def on_device(tokens, cotangent, weight_codes, block_scales, block_index, block_count, ia3_scale):
    m = lax.axis_index("mp")
    pos = jnp.stack([m // (2 * NZ), lax.rem(m // 2, NZ), lax.rem(m, 2)]).astype(jnp.int32)
    block = (256, 128)

    with jax.named_scope("gather"):
        sib_t = swap(tokens)
        sib_c = swap(cotangent)
        chip_t, chip_c, own_c = own(pos, tokens, cotangent, sib_t, sib_c)
        near_t = stack([send(chip_t, dy=1, signed=True), send(tokens, dy=2)])
        t0, t1 = call(merge_t_kernel, "merge_t", (pos, chip_t, near_t, swap(near_t)), [array((4, 256, 128), BF16)] * 2)
        near_c = stack([send(chip_c, dz=d, signed=True) for d in (1, 2, 3)] + [send(own_c, dz=4)], after=(near_t,))
        c0 = call(
            merge_c_kernel, "merge_c", (pos, chip_c, near_c, swap(near_c)), [array((16, 128, 256), BF16)]
        )[0]
        e1 = send(c0, dy=1, signed=True)
        ws = [dequant(h, weight_codes, block_scales, block_index, block_count, (c0,)) for h in range(3)]
        w_gu, w_down, ready = ([w[i] for w in ws] for i in range(3))

        f0, f1, steps = t0, t1, []
        for i in range(3):
            if i == 1:
                f1, ready[0] = lax.optimization_barrier((f1, ready[0]))
            f0 = send(f0, dz=1, signed=True)
            f1 = send(f1, dz=1, signed=True)
            steps.append((f0, f1))
        mine = stack(steps[0] + steps[1])
        ys = (0, 2, -1, 1)
        t_pieces = [t0, t1, mine, swap(mine)]
        t_places = [
            lambda s: ((0, 0), (2, 0)),
            lambda s: ((-1, 0), (1, 0)),
            lambda s: tuple((dy, -n * s) for n in (1, 2) for dy in ys),
            lambda s: tuple((dy, n * s) for n in (1, 2) for dy in ys),
        ]
        gu, _ = gate_up(pos, w_gu, t_pieces, t_places, after=tuple(ready))
        e2 = send(part_of(pos, e1, ()), dy=1, signed=True)
        c_pieces = [c0, e1, swap(e1), e2, swap(e2)]
        dzs = (0, 4, -1, 1, -2, 2, -3, 3)

        def chosen(sel):
            return tuple((2, (1 + sel) // 2 * u + (1 - sel) // 2 * v) for u, v in zip(dzs[:4], dzs[4:]))

        c_places = [
            lambda s: tuple((0, d) for d in dzs),
            lambda s: tuple((-s, d) for d in dzs),
            lambda s: tuple((s, d) for d in dzs),
            lambda s: chosen(s),
            lambda s: chosen(-s),
        ]
        (part,) = hidden(pos, w_down, c_pieces[:3], c_places[:3])
        f4 = send(pick(pos, f0, f1, after=(ready[1], ready[2])), dz=1, signed=True)
        f4, gu, part = lax.optimization_barrier((f4, gu, part))
        mine = stack(steps[2])
        t_pieces = [mine, swap(mine), f4, swap(f4)]
        t_places = [
            lambda s: tuple((dy, -3 * s) for dy in ys),
            lambda s: tuple((dy, 3 * s) for dy in ys),
            lambda s: (((s - 1) // 2, 4), (1 + (s + 1) // 2, 4)),
            lambda s: (((-s - 1) // 2, 4), (1 + (1 - s) // 2, 4)),
        ]
        gu, _ = gate_up(pos, w_gu, t_pieces, t_places, gu, last=True)

        grad, ia3_part = hidden(pos, w_down, c_pieces[3:], c_places[3:], part, gu, ia3_scale[:, None])

    with jax.named_scope("ia3"):
        ia3_part = ia3_part.reshape(384)
        ia3_part = ia3_part + lax.ppermute(ia3_part, "dp", [(0, 1), (1, 0), (2, 3), (3, 2)])
        ia3_grad = ia3_part + lax.ppermute(ia3_part, "dp", [(0, 3), (3, 0), (1, 2), (2, 1)])

    with jax.named_scope("scatter"):
        cuts = ((0, 1, 2, 3), (4, 5, 6, 7))
        ways = ((2, 3, 1, 0), (2, 1, 3, 0))
        orders = [[(dy, dz) for dy in way for dz in dzs] for way, dzs in zip(ways, cuts)]
        sib = [swap(input_part(pos, grad, w_gu, order)[0]) for order in orders]
        a2, a3, a1, a0 = input_part(pos, grad, w_gu, orders[0], sib[0])
        ra2 = send(a2, dy=1)
        ra3 = send(a3, dy=-1)
        b2, b1, b3, b0 = input_part(pos, grad, w_gu, orders[1], sib[1])
        rb2 = send(b2, dy=-1)
        rb1 = send(b1, dy=1)
        ra1 = send(add(a1, ra2), dy=1)
        rb3 = send(add(b3, rb2), dy=-1)
        ra1, ia3_grad = lax.optimization_barrier((ra1, ia3_grad))
        total = call(y_sum_kernel, "y_sum", (pos, a0, ra1, ra3, b0, rb1, rb3), [array((8, 128, 256), BF16)])[0]
        columns = [[dev(y, z, c) for z in range(NZ)] for y in range(NY) for c in range(2)]
        total = lax.all_to_all(total, "mp", 0, 0, axis_index_groups=columns, tiled=True)
        input_grad = call(z_sum_kernel, "z_sum", (total,), [array((256, 128), BF16)])[0]
    return (input_grad, ia3_grad)


def solution(mesh):
    return jax.shard_map(
        on_device,
        mesh=mesh,
        in_specs=(
            P("dp", "mp"),
            P("dp", "mp"),
            P("mp", None, None, None),
            P(None, "mp", None, None),
            P("mp", None),
            P("mp"),
            P("mp"),
        ),
        out_specs=(P("dp", "mp"), P("mp")),
        check_vma=False,
    )
```

```python
import functools

import jax
import jax.numpy as jnp
from jax import lax
from jax.experimental import pallas as pl
from jax.experimental.pallas import tpu as pltpu
from jax.sharding import PartitionSpec as P

NY, NZ = 4, 8
MB = 1 << 20
F32, BF16 = jnp.float32, jnp.bfloat16
VMEM = pl.BlockSpec(memory_space=pltpu.VMEM)
ANY = pl.BlockSpec(memory_space=pl.ANY)
SMEM = pl.BlockSpec(memory_space=pltpu.SMEM)


def dev(y, z, c):
    return ((y % NY) * NZ + z % NZ) * 2 + c


def send(a, dy=0, dz=0, flip=False, signed=False):
    pairs = []
    for y in range(NY):
        for z in range(NZ):
            for c in range(2):
                s = -1 if signed and c else 1
                pairs.append((dev(y, z, c), dev(y + s * dy, z + s * dz, 1 - c if flip else c)))
    return lax.ppermute(a, "mp", pairs)


def swap(a):
    return send(a, flip=True)


def array(shape, dtype):
    return jax.ShapeDtypeStruct(shape, dtype)


FLAG = array((1,), jnp.int32)


def call(kernel, name, ins, outs, scratch=(), limit=6, flops=0, after=(), keep=()):
    def space(a):
        return SMEM if a.dtype == jnp.int32 and a.size < 1024 else VMEM

    skip = len(after) + len(keep)
    size = sum(a.size * a.dtype.itemsize for a in tuple(ins) + tuple(outs))
    return pl.pallas_call(
        (lambda *refs: kernel(*refs[skip:])) if skip else kernel,
        in_specs=[ANY] * len(after) + [VMEM] * len(keep) + [space(a) for a in ins],
        out_specs=[space(a) for a in outs],
        out_shape=list(outs),
        scratch_shapes=list(scratch),
        compiler_params=pltpu.CompilerParams(vmem_limit_bytes=limit * MB),
        cost_estimate=pl.CostEstimate(flops=flops, bytes_accessed=size, transcendentals=0),
        name=name,
    )(*after, *keep, *ins)


CHUNK = 16


def dequant_kernel(h, codes_ref, index_ref, count_ref, scales_ref, gu_ref, down_ref, flag_ref, words, sems):
    flag_ref[0] = 0
    count = count_ref[h]
    cuts = range(0, 48, CHUNK)

    def copy(kc):
        b = kc // CHUNK
        return pltpu.make_async_copy(codes_ref.at[h, pl.ds(kc, CHUNK)], words.at[b], sems.at[b])

    for kc in cuts:
        copy(kc).start()
    gu_ref[...] = jnp.zeros(gu_ref.shape, BF16)
    down_ref[...] = jnp.zeros(down_ref.shape, BF16)
    for kc in cuts:
        copy(kc).wait()

        def slots(s, carry):
            for u in range(4):
                j = 4 * s + u
                k = kc + j
                n = index_ref[h, k]
                live = jnp.where(k < count, 1.0, 0.0).astype(F32)
                coded = words[kc // CHUNK, j] ^ 0x888

                def part(p):
                    v = ((coded << (28 - 4 * p)) >> 28).astype(F32)
                    return (v * (scales_ref[p, h, pl.ds(k, 1), :] * live)).astype(BF16)

                gu_ref[n, :, 0:128] = part(0)
                gu_ref[n, :, 128:256] = part(1)
                down_ref[n] = part(2)
            return carry

        lax.fori_loop(0, jnp.clip((count - kc + 3) // 4, 0, CHUNK // 4), slots, 0)


def dequant(h, codes, scales, index, count, after=()):
    outs = (array((64, 128, 256), BF16), array((64, 128, 128), BF16), FLAG)
    kernel = functools.partial(dequant_kernel, h)
    skip = len(after)
    return pl.pallas_call(
        (lambda *refs: kernel(*refs[skip:])) if skip else kernel,
        in_specs=[ANY] * skip + [ANY, SMEM, SMEM, VMEM],
        out_specs=[VMEM, VMEM, SMEM],
        out_shape=outs,
        scratch_shapes=[pltpu.VMEM((48 // CHUNK, CHUNK, 128, 128), jnp.int32), pltpu.SemaphoreType.DMA((48 // CHUNK,))],
        compiler_params=pltpu.CompilerParams(vmem_limit_bytes=14 * MB),
        cost_estimate=pl.CostEstimate(flops=12_000_000, bytes_accessed=10 * MB, transcendentals=0),
        name="dequant",
    )(*after, codes, index, count, scales)


def chip_of(pos_ref, dy, dz):
    y, z = pos_ref[0], pos_ref[1]
    return lax.rem(y + dy + 2 * NY, NY) * NZ + lax.rem(z + dz + 2 * NZ, NZ)


def chips(pos_ref, places):
    sign = 1 - 2 * pos_ref[2]
    return [chip_of(pos_ref, dy, dz) for place in places for dy, dz in place(sign)]


def own_kernel(tok, cot, sib_t, sib_c, pos_ref, chip_t, chip_c, own_c, tv, cv, sems):
    c = pos_ref[2]
    moves = (
        pltpu.make_async_copy(cot, cv.at[0], sems.at[0]),
        pltpu.make_async_copy(sib_c, cv.at[1], sems.at[1]),
        pltpu.make_async_copy(tok, tv.at[0], sems.at[2]),
        pltpu.make_async_copy(sib_t, tv.at[1], sems.at[3]),
    )
    for move in moves:
        move.start()
    moves[0].wait()
    mine = cv[0].T
    own_c[...] = mine
    chip_c[c] = mine
    moves[1].wait()
    chip_c[1 - c] = cv[1].T
    moves[2].wait()
    chip_t[c] = tv[0]
    moves[3].wait()
    chip_t[1 - c] = tv[1]


def own(pos, tokens, cotangent, sib_t, sib_c):
    return pl.pallas_call(
        own_kernel,
        in_specs=[ANY] * 4 + [SMEM],
        out_specs=[VMEM] * 3,
        out_shape=[array((2, 256, 128), BF16), array((2, 128, 256), BF16), array((128, 256), BF16)],
        scratch_shapes=[
            pltpu.VMEM((2, 256, 128), BF16),
            pltpu.VMEM((2, 256, 128), BF16),
            pltpu.SemaphoreType.DMA((4,)),
        ],
        compiler_params=pltpu.CompilerParams(vmem_limit_bytes=6 * MB),
        cost_estimate=pl.CostEstimate(flops=0, bytes_accessed=MB, transcendentals=0),
        name="own",
    )(tokens, cotangent, sib_t, sib_c, pos)


def stack_kernel(*refs):
    out, at = refs[-1], 0
    for r in refs[:-1]:
        n = r.shape[0] if len(r.shape) == 3 else 1
        out[at : at + n] = r[...].reshape((n,) + r.shape[-2:])
        at += n


def stack(parts, after=()):
    n = sum(p.shape[0] if p.ndim == 3 else 1 for p in parts)
    return call(stack_kernel, "stack", tuple(parts), (array((n,) + parts[0].shape[-2:], BF16),), after=after)[0]


def merge_t_kernel(pos_ref, chip, mine, other, t0, t1):
    c = pos_ref[2]
    t0[0:2] = chip[...]
    t0[2 + c] = mine[2]
    t0[3 - c] = other[2]
    t1[pl.ds(2 * c, 2)] = mine[0:2]
    t1[pl.ds(2 - 2 * c, 2)] = other[0:2]


def merge_c_kernel(pos_ref, chip, mine, other, out):
    c = pos_ref[2]
    out[0:2] = chip[...]
    out[2 + c] = mine[6]
    out[3 - c] = other[6]
    for i in range(3):
        out[pl.ds(4 + 4 * i + 2 * c, 2)] = mine[2 * i : 2 * i + 2]
        out[pl.ds(6 + 4 * i - 2 * c, 2)] = other[2 * i : 2 * i + 2]


def part_kernel(pos_ref, a, out):
    n = out.shape[0]
    out[...] = a[pl.ds(n * pos_ref[2], n)]


def part_of(pos, a, after):
    return call(part_kernel, "part", (pos, a), (array((a.shape[0] // 2,) + a.shape[1:], a.dtype),), after=after, flops=15_000_000_000)[0]


def pick_kernel(pos_ref, a, b, out):
    @pl.when(pos_ref[2] == 0)
    def _():
        out[...] = a[...]

    @pl.when(pos_ref[2] == 1)
    def _():
        out[...] = b[...]


def pick(pos, a, b, after=(), keep=()):
    return call(pick_kernel, "pick", (pos, a, b), (array(a.shape, a.dtype),), after=after, keep=keep)[0]


def gate_up_kernel(places, first, last, pos_ref, w0, w1, w2, *refs):
    pieces = refs[: len(places)]
    rest = refs[len(places) :]
    out_ref, flag_ref = rest[-2], rest[-1]
    flag_ref[0] = 0
    where = chips(pos_ref, places)
    blocks = [piece[i] for piece in pieces for i in range(piece.shape[0])]
    for h, w in enumerate((w0, w1, w2)):
        acc = None if first else rest[0][h]
        for g in range(0, len(where), 8):
            cut = where[g : g + 8]
            lhs = jnp.concatenate(blocks[2 * g : 2 * g + 2 * len(cut)], axis=1)
            rhs = jnp.concatenate([w[pl.ds(2 * j, 2)].reshape(256, 256) for j in cut], axis=0)
            term = jnp.dot(lhs, rhs, preferred_element_type=F32)
            acc = term if acc is None else acc + term
        out_ref[h] = acc.T if last else acc


def gate_up(pos, ws, pieces, places, acc=None, last=False, after=()):
    ins = (pos,) + tuple(ws) + tuple(pieces) + (() if acc is None else (acc,))
    return call(
        functools.partial(gate_up_kernel, places, acc is None, last),
        "gate_up",
        ins,
        (array((3, 256, 256), F32), FLAG),
        limit=24,
        flops=sum(p.shape[0] for p in pieces) * 2 * 256 * 128 * 768,
        after=after,
    )


def hidden_kernel(places, first, last, pos_ref, w0, w1, w2, *refs):
    pieces = refs[: len(places)]
    rest = refs[len(places) :]
    where = chips(pos_ref, places)
    blocks = [piece[i] for piece in pieces for i in range(piece.shape[0])]
    acc = None if first else rest[0][...]
    for g in range(0, len(where), 8):
        cut = where[g : g + 8]
        lhs = jnp.concatenate(
            [jnp.concatenate([w[2 * j + c] for j in cut for c in range(2)], axis=1) for w in (w0, w1, w2)],
            axis=0,
        )
        rhs = jnp.concatenate([blocks[2 * i + c] for i in range(g, g + 8) for c in range(2)], axis=0)
        term = jnp.dot(lhs, rhs, preferred_element_type=F32)
        acc = term if acc is None else acc + term
    if not last:
        rest[-1][...] = acc
        return
    gu_ref, scale_ref, grad_ref, ia3_ref = rest[-4:]
    for h in range(3):
        rows = slice(128 * h, 128 * h + 128)
        hidden = acc[rows]
        gate = gu_ref[h, 0:128]
        up = gu_ref[h, 128:256]
        s = jax.nn.sigmoid(gate)
        activated = gate * s
        ia3_ref[:, rows] = jnp.sum((hidden * activated * up).T, axis=0, keepdims=True)
        scaled = hidden * scale_ref[rows, :]
        grad_ref[h, 0:128] = (scaled * up * s * (1.0 + gate * (1.0 - s))).astype(BF16)
        grad_ref[h, 128:256] = (scaled * activated).astype(BF16)


def hidden(pos, ws, pieces, places, acc=None, gu=None, scale=None):
    last = gu is not None
    ins = (pos,) + tuple(ws) + tuple(pieces) + (() if acc is None else (acc,)) + ((gu, scale) if last else ())
    outs = (array((3, 256, 256), BF16), array((1, 384), F32)) if last else (array((384, 256), F32),)
    return call(
        functools.partial(hidden_kernel, places, acc is None, last),
        "hidden",
        ins,
        outs,
        limit=16,
        flops=sum(p.shape[0] for p in pieces) * 2 * 384 * 128 * 256,
    )


def input_kernel(order, par_of, pos_ref, grad_ref, w0, w1, w2, *refs):
    par = par_of(pos_ref[2])
    where = [2 * chip_of(pos_ref, dy, dz) + par for dy, dz in order]
    added, outs = (refs[0], refs[1:]) if len(refs) > 1 else (None, refs)
    for g in range(0, len(order), 4):
        cut = where[g : g + 4]
        acc = None
        for h, w in enumerate((w0, w1, w2)):
            lhs = jnp.concatenate([w[j] for j in cut], axis=0)
            term = jnp.dot(lhs, grad_ref[h], preferred_element_type=F32)
            acc = term if acc is None else acc + term
        acc = acc.reshape(len(cut), 128, 256)
        if added is not None:
            acc = acc + added[g : g + 4].astype(F32)
            outs[g // 4][...] = acc.astype(outs[g // 4].dtype)
        else:
            outs[0][g : g + 4] = acc.astype(BF16)


def input_part(pos, grad, ws, order, added=None, after=()):
    n = len(order)
    if added is None:
        kernel = functools.partial(input_kernel, order, lambda c: 1 - c)
        outs = [array((n, 128, 256), BF16)]
    else:
        kernel = functools.partial(input_kernel, order, lambda c: c)
        outs = [array((4, 128, 256), BF16)] * (n // 4 - 2) + [array((4, 128, 256), F32)] * 2
    return call(
        kernel,
        "input_away" if added is None else "input_here",
        (pos, grad) + tuple(ws) + (() if added is None else (added,)),
        outs,
        limit=24,
        flops=n * 2 * 128 * 256 * 768,
        after=after,
    )


def add_kernel(a, r, out):
    out[...] = (a[...] + r[...].astype(F32)).astype(BF16)


def add(a, r):
    return call(add_kernel, "add", (a, r), (array(a.shape, BF16),))[0]


def y_sum_kernel(pos_ref, a0, ra1, ra3, b0, rb1, rb3, out):
    for i in range(4):
        for at, v, r, q in ((i, a0, ra1, ra3), (i + 4, b0, rb1, rb3)):
            total = v[i] + (r[i].astype(F32) + q[i].astype(F32))
            out[lax.rem(pos_ref[1] + at, NZ)] = total.astype(BF16)


def z_sum_kernel(parts, out):
    v = parts[0].astype(F32)
    for i in range(1, NZ):
        v = v + parts[i].astype(F32)
    out[...] = v.T.astype(BF16)


def on_device(tokens, cotangent, weight_codes, block_scales, block_index, block_count, ia3_scale):
    m = lax.axis_index("mp")
    pos = jnp.stack([m // (2 * NZ), lax.rem(m // 2, NZ), lax.rem(m, 2)]).astype(jnp.int32)
    block = (256, 128)

    with jax.named_scope("gather"):
        sib_t = swap(tokens)
        sib_c = swap(cotangent)
        chip_t, chip_c, own_c = own(pos, tokens, cotangent, sib_t, sib_c)
        near_t = stack([send(chip_t, dy=1, signed=True), send(tokens, dy=2)])
        t0, t1 = call(merge_t_kernel, "merge_t", (pos, chip_t, near_t, swap(near_t)), [array((4, 256, 128), BF16)] * 2)
        near_c = stack([send(chip_c, dz=d, signed=True) for d in (1, 2, 3)] + [send(own_c, dz=4)], after=(near_t,))
        c0 = call(
            merge_c_kernel, "merge_c", (pos, chip_c, near_c, swap(near_c)), [array((16, 128, 256), BF16)],
            after=(t0,),
        )[0]
        e1 = send(c0, dy=1, signed=True)
        ws = [dequant(h, weight_codes, block_scales, block_index, block_count, (c0,)) for h in range(3)]
        w_gu, w_down, ready = ([w[i] for w in ws] for i in range(3))

        f0, f1, steps = t0, t1, []
        for i in range(3):
            if i == 1:
                f1, ready[0] = lax.optimization_barrier((f1, ready[0]))
            f0 = send(f0, dz=1, signed=True)
            f1 = send(f1, dz=1, signed=True)
            steps.append((f0, f1))
        mine = stack(steps[0] + steps[1])
        ys = (0, 2, -1, 1)
        t_pieces = [t0, t1, mine, swap(mine)]
        t_places = [
            lambda s: ((0, 0), (2, 0)),
            lambda s: ((-1, 0), (1, 0)),
            lambda s: tuple((dy, -n * s) for n in (1, 2) for dy in ys),
            lambda s: tuple((dy, n * s) for n in (1, 2) for dy in ys),
        ]
        gu, _ = gate_up(pos, w_gu, t_pieces, t_places, after=tuple(ready))
        e2 = send(part_of(pos, e1, ()), dy=1, signed=True)
        c_pieces = [c0, e1, swap(e1), e2, swap(e2)]
        dzs = (0, 4, -1, 1, -2, 2, -3, 3)

        def chosen(sel):
            return tuple((2, (1 + sel) // 2 * u + (1 - sel) // 2 * v) for u, v in zip(dzs[:4], dzs[4:]))

        c_places = [
            lambda s: tuple((0, d) for d in dzs),
            lambda s: tuple((-s, d) for d in dzs),
            lambda s: tuple((s, d) for d in dzs),
            lambda s: chosen(s),
            lambda s: chosen(-s),
        ]
        (part,) = hidden(pos, w_down, c_pieces[:3], c_places[:3])
        f4 = send(pick(pos, f0, f1, after=(ready[1], ready[2])), dz=1, signed=True)
        f4, gu, part = lax.optimization_barrier((f4, gu, part))
        mine = stack(steps[2])
        t_pieces = [mine, swap(mine), f4, swap(f4)]
        t_places = [
            lambda s: tuple((dy, -3 * s) for dy in ys),
            lambda s: tuple((dy, 3 * s) for dy in ys),
            lambda s: (((s - 1) // 2, 4), (1 + (s + 1) // 2, 4)),
            lambda s: (((-s - 1) // 2, 4), (1 + (1 - s) // 2, 4)),
        ]
        gu, _ = gate_up(pos, w_gu, t_pieces, t_places, gu, last=True)

        grad, ia3_part = hidden(pos, w_down, c_pieces[3:], c_places[3:], part, gu, ia3_scale[:, None])

    with jax.named_scope("ia3"):
        ia3_part = ia3_part.reshape(384)
        ia3_part = ia3_part + lax.ppermute(ia3_part, "dp", [(0, 1), (1, 0), (2, 3), (3, 2)])
        ia3_grad = ia3_part + lax.ppermute(ia3_part, "dp", [(0, 3), (3, 0), (1, 2), (2, 1)])

    with jax.named_scope("scatter"):
        cuts = ((0, 1, 2, 3), (4, 5, 6, 7))
        ways = ((2, 3, 1, 0), (2, 1, 3, 0))
        orders = [[(dy, dz) for dy in way for dz in dzs] for way, dzs in zip(ways, cuts)]
        sib = [swap(input_part(pos, grad, w_gu, order)[0]) for order in orders]
        a2, a3, a1, a0 = input_part(pos, grad, w_gu, orders[0], sib[0])
        ra2 = send(a2, dy=1)
        ra3 = send(a3, dy=-1)
        b2, b1, b3, b0 = input_part(pos, grad, w_gu, orders[1], sib[1])
        rb2 = send(b2, dy=-1)
        rb1 = send(b1, dy=1)
        ra1 = send(add(a1, ra2), dy=1)
        rb3 = send(add(b3, rb2), dy=-1)
        ra1, ia3_grad = lax.optimization_barrier((ra1, ia3_grad))
        total = call(y_sum_kernel, "y_sum", (pos, a0, ra1, ra3, b0, rb1, rb3), [array((8, 128, 256), BF16)])[0]
        columns = [[dev(y, z, c) for z in range(NZ)] for y in range(NY) for c in range(2)]
        total = lax.all_to_all(total, "mp", 0, 0, axis_index_groups=columns, tiled=True)
        input_grad = call(z_sum_kernel, "z_sum", (total,), [array((256, 128), BF16)])[0]
    return (input_grad, ia3_grad)


def solution(mesh):
    return jax.shard_map(
        on_device,
        mesh=mesh,
        in_specs=(
            P("dp", "mp"),
            P("dp", "mp"),
            P("mp", None, None, None),
            P(None, "mp", None, None),
            P("mp", None),
            P("mp"),
            P("mp"),
        ),
        out_specs=(P("dp", "mp"), P("mp")),
        check_vma=False,
    )
```

```python
import functools

import jax
import jax.numpy as jnp
from jax import lax
from jax.experimental import pallas as pl
from jax.experimental.pallas import tpu as pltpu
from jax.sharding import PartitionSpec as P

NY, NZ = 4, 8
MB = 1 << 20
F32, BF16 = jnp.float32, jnp.bfloat16
VMEM = pl.BlockSpec(memory_space=pltpu.VMEM)
ANY = pl.BlockSpec(memory_space=pl.ANY)
SMEM = pl.BlockSpec(memory_space=pltpu.SMEM)


def dev(y, z, c):
    return ((y % NY) * NZ + z % NZ) * 2 + c


def send(a, dy=0, dz=0, flip=False, signed=False):
    pairs = []
    for y in range(NY):
        for z in range(NZ):
            for c in range(2):
                s = -1 if signed and c else 1
                pairs.append((dev(y, z, c), dev(y + s * dy, z + s * dz, 1 - c if flip else c)))
    return lax.ppermute(a, "mp", pairs)


def swap(a):
    return send(a, flip=True)


def array(shape, dtype):
    return jax.ShapeDtypeStruct(shape, dtype)


FLAG = array((1,), jnp.int32)


def call(kernel, name, ins, outs, scratch=(), limit=6, flops=0, after=(), keep=()):
    def space(a):
        return SMEM if a.dtype == jnp.int32 and a.size < 1024 else VMEM

    skip = len(after) + len(keep)
    size = sum(a.size * a.dtype.itemsize for a in tuple(ins) + tuple(outs))
    return pl.pallas_call(
        (lambda *refs: kernel(*refs[skip:])) if skip else kernel,
        in_specs=[ANY] * len(after) + [VMEM] * len(keep) + [space(a) for a in ins],
        out_specs=[space(a) for a in outs],
        out_shape=list(outs),
        scratch_shapes=list(scratch),
        compiler_params=pltpu.CompilerParams(vmem_limit_bytes=limit * MB),
        cost_estimate=pl.CostEstimate(flops=flops, bytes_accessed=size, transcendentals=0),
        name=name,
    )(*after, *keep, *ins)


CHUNK = 16


def dequant_kernel(h, codes_ref, index_ref, count_ref, scales_ref, gu_ref, down_ref, flag_ref, words, sems):
    flag_ref[0] = 0
    count = count_ref[h]
    cuts = range(0, 48, CHUNK)

    def copy(kc):
        b = kc // CHUNK
        return pltpu.make_async_copy(codes_ref.at[h, pl.ds(kc, CHUNK)], words.at[b], sems.at[b])

    for kc in cuts:
        copy(kc).start()
    gu_ref[...] = jnp.zeros(gu_ref.shape, BF16)
    down_ref[...] = jnp.zeros(down_ref.shape, BF16)
    for kc in cuts:
        copy(kc).wait()

        def slots(s, carry):
            for u in range(4):
                j = 4 * s + u
                k = kc + j
                n = index_ref[h, k]
                live = jnp.where(k < count, 1.0, 0.0).astype(F32)
                coded = words[kc // CHUNK, j] ^ 0x888

                def part(p):
                    v = ((coded << (28 - 4 * p)) >> 28).astype(F32)
                    return (v * (scales_ref[p, h, pl.ds(k, 1), :] * live)).astype(BF16)

                gu_ref[n, :, 0:128] = part(0)
                gu_ref[n, :, 128:256] = part(1)
                down_ref[n] = part(2)
            return carry

        lax.fori_loop(0, jnp.clip((count - kc + 3) // 4, 0, CHUNK // 4), slots, 0)


def dequant(h, codes, scales, index, count, after=()):
    outs = (array((64, 128, 256), BF16), array((64, 128, 128), BF16), FLAG)
    kernel = functools.partial(dequant_kernel, h)
    skip = len(after)
    return pl.pallas_call(
        (lambda *refs: kernel(*refs[skip:])) if skip else kernel,
        in_specs=[ANY] * skip + [ANY, SMEM, SMEM, VMEM],
        out_specs=[VMEM, VMEM, SMEM],
        out_shape=outs,
        scratch_shapes=[pltpu.VMEM((48 // CHUNK, CHUNK, 128, 128), jnp.int32), pltpu.SemaphoreType.DMA((48 // CHUNK,))],
        compiler_params=pltpu.CompilerParams(vmem_limit_bytes=14 * MB),
        cost_estimate=pl.CostEstimate(flops=12_000_000, bytes_accessed=10 * MB, transcendentals=0),
        name="dequant",
    )(*after, codes, index, count, scales)


def chip_of(pos_ref, dy, dz):
    y, z = pos_ref[0], pos_ref[1]
    return lax.rem(y + dy + 2 * NY, NY) * NZ + lax.rem(z + dz + 2 * NZ, NZ)


def chips(pos_ref, places):
    sign = 1 - 2 * pos_ref[2]
    return [chip_of(pos_ref, dy, dz) for place in places for dy, dz in place(sign)]


def own_kernel(tok, cot, sib_t, sib_c, pos_ref, chip_t, chip_c, own_c, tv, cv, sems):
    c = pos_ref[2]
    moves = (
        pltpu.make_async_copy(cot, cv.at[0], sems.at[0]),
        pltpu.make_async_copy(sib_c, cv.at[1], sems.at[1]),
        pltpu.make_async_copy(tok, tv.at[0], sems.at[2]),
        pltpu.make_async_copy(sib_t, tv.at[1], sems.at[3]),
    )
    for move in moves:
        move.start()
    moves[0].wait()
    mine = cv[0].T
    own_c[...] = mine
    chip_c[c] = mine
    moves[1].wait()
    chip_c[1 - c] = cv[1].T
    moves[2].wait()
    chip_t[c] = tv[0]
    moves[3].wait()
    chip_t[1 - c] = tv[1]


def own(pos, tokens, cotangent, sib_t, sib_c):
    return pl.pallas_call(
        own_kernel,
        in_specs=[ANY] * 4 + [SMEM],
        out_specs=[VMEM] * 3,
        out_shape=[array((2, 256, 128), BF16), array((2, 128, 256), BF16), array((128, 256), BF16)],
        scratch_shapes=[
            pltpu.VMEM((2, 256, 128), BF16),
            pltpu.VMEM((2, 256, 128), BF16),
            pltpu.SemaphoreType.DMA((4,)),
        ],
        compiler_params=pltpu.CompilerParams(vmem_limit_bytes=6 * MB),
        cost_estimate=pl.CostEstimate(flops=0, bytes_accessed=MB, transcendentals=0),
        name="own",
    )(tokens, cotangent, sib_t, sib_c, pos)


def stack_kernel(*refs):
    out, at = refs[-1], 0
    for r in refs[:-1]:
        n = r.shape[0] if len(r.shape) == 3 else 1
        out[at : at + n] = r[...].reshape((n,) + r.shape[-2:])
        at += n


def stack(parts, after=()):
    n = sum(p.shape[0] if p.ndim == 3 else 1 for p in parts)
    return call(stack_kernel, "stack", tuple(parts), (array((n,) + parts[0].shape[-2:], BF16),), after=after)[0]


def merge_t_kernel(pos_ref, chip, mine, other, t0, t1):
    c = pos_ref[2]
    t0[0:2] = chip[...]
    t0[2 + c] = mine[2]
    t0[3 - c] = other[2]
    t1[pl.ds(2 * c, 2)] = mine[0:2]
    t1[pl.ds(2 - 2 * c, 2)] = other[0:2]


def merge_c_kernel(pos_ref, chip, mine, other, out):
    c = pos_ref[2]
    out[0:2] = chip[...]
    out[2 + c] = mine[6]
    out[3 - c] = other[6]
    for i in range(3):
        out[pl.ds(4 + 4 * i + 2 * c, 2)] = mine[2 * i : 2 * i + 2]
        out[pl.ds(6 + 4 * i - 2 * c, 2)] = other[2 * i : 2 * i + 2]


def part_kernel(pos_ref, a, out):
    n = out.shape[0]
    out[...] = a[pl.ds(n * pos_ref[2], n)]


def part_of(pos, a, after):
    return call(part_kernel, "part", (pos, a), (array((a.shape[0] // 2,) + a.shape[1:], a.dtype),), after=after, flops=15_000_000_000)[0]


def pick_kernel(pos_ref, a, b, out):
    @pl.when(pos_ref[2] == 0)
    def _():
        out[...] = a[...]

    @pl.when(pos_ref[2] == 1)
    def _():
        out[...] = b[...]


def pick(pos, a, b, after=(), keep=()):
    return call(pick_kernel, "pick", (pos, a, b), (array(a.shape, a.dtype),), after=after, keep=keep)[0]


def gate_up_kernel(places, first, last, pos_ref, w0, w1, w2, *refs):
    pieces = refs[: len(places)]
    rest = refs[len(places) :]
    out_ref, flag_ref = rest[-2], rest[-1]
    flag_ref[0] = 0
    where = chips(pos_ref, places)
    blocks = [piece[i] for piece in pieces for i in range(piece.shape[0])]
    for h, w in enumerate((w0, w1, w2)):
        acc = None if first else rest[0][h]
        for g in range(0, len(where), 8):
            cut = where[g : g + 8]
            lhs = jnp.concatenate(blocks[2 * g : 2 * g + 2 * len(cut)], axis=1)
            rhs = jnp.concatenate([w[pl.ds(2 * j, 2)].reshape(256, 256) for j in cut], axis=0)
            term = jnp.dot(lhs, rhs, preferred_element_type=F32)
            acc = term if acc is None else acc + term
        out_ref[h] = acc.T if last else acc


def gate_up(pos, ws, pieces, places, acc=None, last=False, after=()):
    ins = (pos,) + tuple(ws) + tuple(pieces) + (() if acc is None else (acc,))
    return call(
        functools.partial(gate_up_kernel, places, acc is None, last),
        "gate_up",
        ins,
        (array((3, 256, 256), F32), FLAG),
        limit=24,
        flops=sum(p.shape[0] for p in pieces) * 2 * 256 * 128 * 768,
        after=after,
    )


def hidden_kernel(places, first, last, pos_ref, w0, w1, w2, *refs):
    pieces = refs[: len(places)]
    rest = refs[len(places) :]
    where = chips(pos_ref, places)
    blocks = [piece[i] for piece in pieces for i in range(piece.shape[0])]
    acc = None if first else rest[0][...]
    for g in range(0, len(where), 8):
        cut = where[g : g + 8]
        lhs = jnp.concatenate(
            [jnp.concatenate([w[2 * j + c] for j in cut for c in range(2)], axis=1) for w in (w0, w1, w2)],
            axis=0,
        )
        rhs = jnp.concatenate([blocks[2 * i + c] for i in range(g, g + 8) for c in range(2)], axis=0)
        term = jnp.dot(lhs, rhs, preferred_element_type=F32)
        acc = term if acc is None else acc + term
    if not last:
        rest[-1][...] = acc
        return
    gu_ref, scale_ref, grad_ref, ia3_ref = rest[-4:]
    for h in range(3):
        rows = slice(128 * h, 128 * h + 128)
        hidden = acc[rows]
        gate = gu_ref[h, 0:128]
        up = gu_ref[h, 128:256]
        s = jax.nn.sigmoid(gate)
        activated = gate * s
        ia3_ref[:, rows] = jnp.sum((hidden * activated * up).T, axis=0, keepdims=True)
        scaled = hidden * scale_ref[rows, :]
        grad_ref[h, 0:128] = (scaled * up * s * (1.0 + gate * (1.0 - s))).astype(BF16)
        grad_ref[h, 128:256] = (scaled * activated).astype(BF16)


def hidden(pos, ws, pieces, places, acc=None, gu=None, scale=None):
    last = gu is not None
    ins = (pos,) + tuple(ws) + tuple(pieces) + (() if acc is None else (acc,)) + ((gu, scale) if last else ())
    outs = (array((3, 256, 256), BF16), array((1, 384), F32)) if last else (array((384, 256), F32),)
    return call(
        functools.partial(hidden_kernel, places, acc is None, last),
        "hidden",
        ins,
        outs,
        limit=16,
        flops=sum(p.shape[0] for p in pieces) * 2 * 384 * 128 * 256,
    )


def input_kernel(order, par_of, pos_ref, grad_ref, w0, w1, w2, *refs):
    par = par_of(pos_ref[2])
    where = [2 * chip_of(pos_ref, dy, dz) + par for dy, dz in order]
    added, outs = (refs[0], refs[1:]) if len(refs) > 1 else (None, refs)
    for g in range(0, len(order), 4):
        cut = where[g : g + 4]
        acc = None
        for h, w in enumerate((w0, w1, w2)):
            lhs = jnp.concatenate([w[j] for j in cut], axis=0)
            term = jnp.dot(lhs, grad_ref[h], preferred_element_type=F32)
            acc = term if acc is None else acc + term
        acc = acc.reshape(len(cut), 128, 256)
        if added is not None:
            acc = acc + added[g : g + 4].astype(F32)
            outs[g // 4][...] = acc.astype(outs[g // 4].dtype)
        else:
            outs[0][g : g + 4] = acc.astype(BF16)


def input_part(pos, grad, ws, order, added=None, after=()):
    n = len(order)
    if added is None:
        kernel = functools.partial(input_kernel, order, lambda c: 1 - c)
        outs = [array((n, 128, 256), BF16)]
    else:
        kernel = functools.partial(input_kernel, order, lambda c: c)
        outs = [array((4, 128, 256), BF16)] * (n // 4 - 2) + [array((4, 128, 256), F32)] * 2
    return call(
        kernel,
        "input_away" if added is None else "input_here",
        (pos, grad) + tuple(ws) + (() if added is None else (added,)),
        outs,
        limit=24,
        flops=n * 2 * 128 * 256 * 768,
        after=after,
    )


def add_kernel(a, r, out):
    out[...] = (a[...] + r[...].astype(F32)).astype(BF16)


def add(a, r):
    return call(add_kernel, "add", (a, r), (array(a.shape, BF16),))[0]


def y_sum_kernel(pos_ref, a0, ra1, ra3, b0, rb1, rb3, out):
    for i in range(4):
        for at, v, r, q in ((i, a0, ra1, ra3), (i + 4, b0, rb1, rb3)):
            total = v[i] + (r[i].astype(F32) + q[i].astype(F32))
            out[lax.rem(pos_ref[1] + at, NZ)] = total.astype(BF16)


def z_sum_kernel(parts, out):
    v = parts[0].astype(F32)
    for i in range(1, NZ):
        v = v + parts[i].astype(F32)
    out[...] = v.T.astype(BF16)


def on_device(tokens, cotangent, weight_codes, block_scales, block_index, block_count, ia3_scale):
    m = lax.axis_index("mp")
    pos = jnp.stack([m // (2 * NZ), lax.rem(m // 2, NZ), lax.rem(m, 2)]).astype(jnp.int32)
    block = (256, 128)

    with jax.named_scope("gather"):
        sib_t = swap(tokens)
        sib_c = swap(cotangent)
        chip_t, chip_c, own_c = own(pos, tokens, cotangent, sib_t, sib_c)
        near_t = stack([send(chip_t, dy=1, signed=True), send(tokens, dy=2)], after=(weight_codes,))
        t0, t1 = call(merge_t_kernel, "merge_t", (pos, chip_t, near_t, swap(near_t)), [array((4, 256, 128), BF16)] * 2)
        near_c = stack([send(chip_c, dz=d, signed=True) for d in (1, 2, 3)] + [send(own_c, dz=4)], after=(near_t, weight_codes))
        c0 = call(
            merge_c_kernel, "merge_c", (pos, chip_c, near_c, swap(near_c)), [array((16, 128, 256), BF16)],
            after=(t0,),
        )[0]
        e1 = send(c0, dy=1, signed=True)
        ws = [dequant(h, weight_codes, block_scales, block_index, block_count, (c0,)) for h in range(3)]
        w_gu, w_down, ready = ([w[i] for w in ws] for i in range(3))

        f0, f1, steps = t0, t1, []
        for i in range(3):
            if i == 1:
                f1, ready[0] = lax.optimization_barrier((f1, ready[0]))
            f0 = send(f0, dz=1, signed=True)
            f1 = send(f1, dz=1, signed=True)
            steps.append((f0, f1))
        mine = stack(steps[0] + steps[1])
        ys = (0, 2, -1, 1)
        t_pieces = [t0, t1, mine, swap(mine)]
        t_places = [
            lambda s: ((0, 0), (2, 0)),
            lambda s: ((-1, 0), (1, 0)),
            lambda s: tuple((dy, -n * s) for n in (1, 2) for dy in ys),
            lambda s: tuple((dy, n * s) for n in (1, 2) for dy in ys),
        ]
        gu, _ = gate_up(pos, w_gu, t_pieces, t_places, after=tuple(ready))
        e2 = send(part_of(pos, e1, ()), dy=1, signed=True)
        c_pieces = [c0, e1, swap(e1), e2, swap(e2)]
        dzs = (0, 4, -1, 1, -2, 2, -3, 3)

        def chosen(sel):
            return tuple((2, (1 + sel) // 2 * u + (1 - sel) // 2 * v) for u, v in zip(dzs[:4], dzs[4:]))

        c_places = [
            lambda s: tuple((0, d) for d in dzs),
            lambda s: tuple((-s, d) for d in dzs),
            lambda s: tuple((s, d) for d in dzs),
            lambda s: chosen(s),
            lambda s: chosen(-s),
        ]
        (part,) = hidden(pos, w_down, c_pieces[:3], c_places[:3])
        f4 = send(pick(pos, f0, f1, after=(ready[1], ready[2])), dz=1, signed=True)
        f4, gu, part = lax.optimization_barrier((f4, gu, part))
        mine = stack(steps[2])
        t_pieces = [mine, swap(mine), f4, swap(f4)]
        t_places = [
            lambda s: tuple((dy, -3 * s) for dy in ys),
            lambda s: tuple((dy, 3 * s) for dy in ys),
            lambda s: (((s - 1) // 2, 4), (1 + (s + 1) // 2, 4)),
            lambda s: (((-s - 1) // 2, 4), (1 + (1 - s) // 2, 4)),
        ]
        gu, _ = gate_up(pos, w_gu, t_pieces, t_places, gu, last=True)

        grad, ia3_part = hidden(pos, w_down, c_pieces[3:], c_places[3:], part, gu, ia3_scale[:, None])

    with jax.named_scope("ia3"):
        ia3_part = ia3_part.reshape(384)
        ia3_part = ia3_part + lax.ppermute(ia3_part, "dp", [(0, 1), (1, 0), (2, 3), (3, 2)])
        ia3_grad = ia3_part + lax.ppermute(ia3_part, "dp", [(0, 3), (3, 0), (1, 2), (2, 1)])

    with jax.named_scope("scatter"):
        cuts = ((0, 1, 2, 3), (4, 5, 6, 7))
        ways = ((2, 3, 1, 0), (2, 1, 3, 0))
        orders = [[(dy, dz) for dy in way for dz in dzs] for way, dzs in zip(ways, cuts)]
        sib = [swap(input_part(pos, grad, w_gu, order)[0]) for order in orders]
        a2, a3, a1, a0 = input_part(pos, grad, w_gu, orders[0], sib[0])
        ra2 = send(a2, dy=1)
        ra3 = send(a3, dy=-1)
        b2, b1, b3, b0 = input_part(pos, grad, w_gu, orders[1], sib[1])
        rb2 = send(b2, dy=-1)
        rb1 = send(b1, dy=1)
        ra1 = send(add(a1, ra2), dy=1)
        rb3 = send(add(b3, rb2), dy=-1)
        ra1, ia3_grad = lax.optimization_barrier((ra1, ia3_grad))
        total = call(y_sum_kernel, "y_sum", (pos, a0, ra1, ra3, b0, rb1, rb3), [array((8, 128, 256), BF16)])[0]
        columns = [[dev(y, z, c) for z in range(NZ)] for y in range(NY) for c in range(2)]
        total = lax.all_to_all(total, "mp", 0, 0, axis_index_groups=columns, tiled=True)
        input_grad = call(z_sum_kernel, "z_sum", (total,), [array((256, 128), BF16)])[0]
    return (input_grad, ia3_grad)


def solution(mesh):
    return jax.shard_map(
        on_device,
        mesh=mesh,
        in_specs=(
            P("dp", "mp"),
            P("dp", "mp"),
            P("mp", None, None, None),
            P(None, "mp", None, None),
            P("mp", None),
            P("mp"),
            P("mp"),
        ),
        out_specs=(P("dp", "mp"), P("mp")),
        check_vma=False,
    )
```
